32 devices in a mesh: expert: 8 (over z, x), tensor: 4 (over y, core).
Axes of the slice: x: 2, y: 2, z: 4, core: 2. Of those that a mesh axis runs over, the one named last changes fastest.
Arguments:
- tokens: bfloat16 [256, 4096], P('expert', 'tensor'), may hold values from -6 to 6
- cotangent: bfloat16 [256, 4096], P('expert', 'tensor'), may hold values from -6 to 6
- routing: int32 [256, 8], P('expert'), may hold values from 0 to 63, as said below
- gates: float32 [256, 8], P('expert'), may hold values from 0.1 to 0.4
- w_in: bfloat16 [64, 4096, 1536], P('expert', None, 'tensor'), may hold values from -0.09375 to 0.09375
- w_out: bfloat16 [64, 1536, 4096], P('expert', 'tensor'), may hold values from -0.15625 to 0.15625
Outputs:
- mixed: bfloat16 [256, 4096], P('expert', 'tensor')
- d_tokens: bfloat16 [256, 4096], P('expert', 'tensor')
- d_w_in: bfloat16 [64, 4096, 1536], P('expert', None, 'tensor')
- d_w_out: bfloat16 [64, 1536, 4096], P('expert', 'tensor')
The draws below stay inside these ranges and needn't reach their ends.
Inputs may be any that keep to these rules, and one draw needn't show every extreme that they name: `routing`: each row names 8 different experts. In each aligned block of 32 rows (the tokens of one index of the expert axis) no expert is named by more than 8 rows, and one expert is named by exactly 8 rows of every block.
All inputs are finite; a program needn't handle non-finite values.
Results may differ from the reference program's by a relative error of at most 0.0058.
Values may be sent and summed in bfloat16 or wider, within the bound.
No kernel may reach another device: no remote copies, remote signals or barrier semaphores. Data moves between devices by JAX's collectives and lax.ppermute only.
A program may use at most 192 MiB of HBM per device.

```python
import jax
import jax.numpy as jnp
from jax import lax

D = 4096
FF = 1536
EXPERTS = 64
TOP = 8
TOK_DEV = 32
SLOT = 8
TOKENS = 256


def draw_routing(key, part):
    block_count = TOKENS // TOK_DEV
    busy_key, rest_key = jax.random.split(key)
    busiest = jax.random.randint(busy_key, (), 0, EXPERTS, dtype=jnp.int32)
    columns = jnp.arange(TOP, dtype=jnp.int32)

    def one_block(block_key):
        subkeys = jax.random.split(block_key, 4)
        shuffled = jax.random.permutation(subkeys[0], TOK_DEV).astype(jnp.int32)
        inverse = jnp.zeros((TOK_DEV,), jnp.int32).at[shuffled].set(jnp.arange(TOK_DEV, dtype=jnp.int32))
        is_busy = (inverse < SLOT).astype(jnp.int32)
        others = jax.random.permutation(subkeys[1], EXPERTS - 1).astype(jnp.int32)
        others = others + (others >= busiest).astype(jnp.int32)
        period = jax.random.randint(subkeys[2], (), 4 * TOP, EXPERTS, dtype=jnp.int32)
        demand = TOP - is_busy
        offset = (jnp.cumsum(demand) - demand).astype(jnp.int32)
        position = offset[:, None] + columns[None, :] - is_busy[:, None]
        chosen = others[jnp.mod(position, period)]
        chosen = jnp.where((is_busy[:, None] == 1) & (columns[None, :] == 0), busiest, chosen)
        rotation = jax.random.randint(subkeys[3], (TOK_DEV,), 0, TOP, dtype=jnp.int32)
        rolled = jnp.mod(columns[None, :] + rotation[:, None], TOP)
        return jnp.take_along_axis(chosen, rolled, axis=1)
    blocks = jax.vmap(one_block)(jax.random.split(rest_key, block_count))
    return blocks.reshape(TOKENS, TOP).astype(jnp.int32)


def level_of(own_key, shape, cuts, low, high):
    factor_of = 1.0
    for dim, shards_of in cuts:
        steps = jax.random.uniform(jax.random.fold_in(jax.random.fold_in(own_key, 6), dim), (shards_of,), jnp.float32, low / len(cuts), high / len(cuts))
        factor_of = factor_of * jnp.repeat(jnp.exp(steps), shape[dim] // shards_of).reshape((-1,) + (1,) * (len(shape) - 1 - dim))
    return factor_of


def gaussian(own_key, extent, width, reach, cuts=(), kind=jnp.bfloat16):
    drawn = jax.random.normal(own_key, extent, jnp.float32) * width
    if len(cuts) > 0:
        drawn = level_of(own_key, extent, cuts, -0.22, 0.18) * drawn
    return jnp.clip(drawn, min=-reach, max=reach).astype(kind)


def setup_inputs(seed: int = 0) -> dict:
    key_of = jax.random.split(jax.random.key(seed), 7)
    return {
        "tokens": gaussian(key_of[0], (TOKENS, D), 1.0, 6.0, ((0, 8), (1, 4))),
        "cotangent": gaussian(key_of[1], (TOKENS, D), 1.0, 6.0, ((0, 8), (1, 4))),
        "routing": draw_routing(jax.random.fold_in(key_of[6], 71), 0),
        "gates": jnp.clip(0.1 + 0.3 * jax.random.uniform(key_of[3], (TOKENS, TOP), jnp.float32) ** level_of(key_of[3], (TOKENS, TOP), ((0, 8),), -0.2, 0.2), 0.1, 0.4),
        "w_in": gaussian(key_of[4], (EXPERTS, D, FF), D ** -0.5, 0.09375, ((0, 8), (2, 4))),
        "w_out": gaussian(key_of[5], (EXPERTS, FF, D), FF ** -0.5, 0.15625, ((0, 8), (1, 4))),
    }


row_tile = 64


def reference(tokens, cotangent, routing, gates, w_in, w_out):
    pair_total = TOKENS * TOP
    flat_routes = routing.reshape(-1).astype(jnp.int32)
    sorted_pairs = jnp.argsort(flat_routes, stable=True).astype(jnp.int32)
    expert_load = jnp.sum((flat_routes[None, :] == jnp.arange(EXPERTS, dtype=jnp.int32)[:, None]).astype(jnp.int32), axis=1).astype(jnp.int32)
    row_first = (jnp.cumsum(expert_load) - expert_load).astype(jnp.int32)
    padded_pairs = jnp.concatenate([sorted_pairs, jnp.zeros((row_tile,), jnp.int32)])
    gate_flat = gates.reshape(-1)

    def expert_step(carry, inputs):
        out_pairs, grad_pairs = carry
        weight_in, weight_out, first_row, row_count = inputs

        def tile_step(tile, state):
            out_acc, grad_acc, grad_in, grad_out = state
            offset = (first_row + tile * row_tile).astype(jnp.int32)
            pair_ids = lax.dynamic_slice(padded_pairs, (offset,), (row_tile,))
            usable = (jnp.arange(row_tile, dtype=jnp.int32) + tile * row_tile) < row_count
            token_rows = pair_ids // TOP
            inputs_tile = jnp.where(usable[:, None], tokens[token_rows], jnp.zeros((), tokens.dtype)).astype(tokens.dtype)
            gate_rows = jnp.where(usable, gate_flat[pair_ids], jnp.zeros((), jnp.float32))
            scaled_cot = (gate_rows[:, None] * cotangent[token_rows].astype(jnp.float32)).astype(jnp.bfloat16)
            preact = jnp.dot(inputs_tile, weight_in, preferred_element_type=jnp.float32)
            sigmoid_val = jax.nn.sigmoid(preact)
            hidden = (preact * sigmoid_val).astype(jnp.bfloat16)
            outputs = jnp.dot(hidden, weight_out, preferred_element_type=jnp.float32)
            grad_hidden = jnp.dot(scaled_cot, weight_out.T, preferred_element_type=jnp.float32)
            grad_preact = (grad_hidden * sigmoid_val * (1.0 + preact * (1.0 - sigmoid_val))).astype(jnp.bfloat16)
            grad_rows = jnp.dot(grad_preact, weight_in.T, preferred_element_type=jnp.float32)
            grad_out = grad_out + jnp.dot(hidden.T, scaled_cot, preferred_element_type=jnp.float32)
            grad_in = grad_in + jnp.dot(inputs_tile.T, grad_preact, preferred_element_type=jnp.float32)
            out_acc = out_acc.at[pair_ids].add(jnp.where(usable[:, None], outputs, jnp.zeros((), jnp.float32)))
            grad_acc = grad_acc.at[pair_ids].add(jnp.where(usable[:, None], grad_rows, jnp.zeros((), jnp.float32)))
            return out_acc, grad_acc, grad_in, grad_out

        tile_count = ((row_count + row_tile - 1) // row_tile).astype(jnp.int32)
        start_state = (out_pairs, grad_pairs, jnp.zeros((D, FF), jnp.float32), jnp.zeros((FF, D), jnp.float32))
        result = lax.fori_loop(jnp.zeros((), jnp.int32), tile_count, tile_step, start_state)
        return (result[0], result[1]), (result[2].astype(jnp.bfloat16), result[3].astype(jnp.bfloat16))

    start_carry = (jnp.zeros((pair_total, D), jnp.float32), jnp.zeros((pair_total, D), jnp.float32))
    (out_pairs, grad_pairs), (d_w_in, d_w_out) = lax.scan(expert_step, start_carry, (w_in, w_out, row_first, expert_load))
    mixed = jnp.sum(gates[:, :, None] * out_pairs.reshape(TOKENS, TOP, D), axis=1).astype(jnp.bfloat16)
    d_tokens = jnp.sum(grad_pairs.reshape(TOKENS, TOP, D), axis=1).astype(jnp.bfloat16)
    return (mixed, d_tokens, d_w_in, d_w_out)
```

```python
import functools

import jax
import jax.numpy as jnp
from jax import lax
from jax.experimental import pallas as pl
from jax.experimental.pallas import tpu as pltpu
from jax.sharding import PartitionSpec as P

MIB = 1024 * 1024
LIMIT = 40 * MIB
DIRECT = 8
F32 = jnp.float32
BF16 = jnp.bfloat16


def swap(value, axis, bits):
    size = lax.axis_size(axis)
    return lax.ppermute(value, axis, [(i, i ^ bits) for i in range(size)])


def gather_rows(value):
    size = lax.axis_size("expert")
    if size > DIRECT:
        return lax.all_gather(value, "expert", axis=0, tiled=True)
    return jnp.concatenate([value] + [swap(value, "expert", s) for s in range(1, size)], axis=0)


def scatter_rows(value, rows):
    size = lax.axis_size("expert")
    if size > DIRECT:
        return lax.psum_scatter(value.astype(F32), "expert", scatter_dimension=0, tiled=True)
    total = value[:rows].astype(F32)
    for s in range(1, size):
        total = total + swap(value[s * rows : (s + 1) * rows], "expert", s).astype(F32)
    return total


def gather_chunks(value):
    chunks = {0: value}
    bit = lax.axis_size("tensor") // 2
    while bit:
        chunks.update({s | bit: swap(c, "tensor", bit) for s, c in list(chunks.items())})
        bit //= 2
    return [chunks[s] for s in range(len(chunks))]


def scatter_chunks(even, odd):
    size = lax.axis_size("tensor")
    got = swap(odd, "tensor", 1)
    parts = [even[i].astype(F32) + got[i].astype(F32) for i in range(size // 2)]
    bit = 2
    while bit < size:
        kept = []
        for i in range(len(parts) // 2):
            sent = parts[2 * i + 1].astype(BF16)
            kept.append(parts[2 * i] + swap(sent, "tensor", bit).astype(F32))
        parts = kept
        bit *= 2
    return parts[0].astype(BF16)


def column(gates, index):
    lane = lax.broadcasted_iota(jnp.int32, gates.shape, 1)
    return jnp.sum(jnp.where(lane == index, gates, 0.0), axis=1, keepdims=True)


def place(me_ref, s, width):
    return pl.ds(pl.multiple_of((me_ref[0] ^ s) * width, width), width)


def dot(a, b, dims=((1,), (0,))):
    return lax.dot_general(a, b, (dims, ((), ())), preferred_element_type=F32)


def preact_kernel(n, me_ref, gates_ref, *refs):
    xs, (w_ref, act_ref, slope_ref) = refs[:n], refs[n:]
    width = xs[0].shape[1]
    pre = sum(dot(xs[s][...], w_ref[0, place(me_ref, s, width), :]) for s in range(n))
    sig = jax.nn.sigmoid(pre)
    gate = column(gates_ref[...], pl.program_id(0))
    act_ref[...] = (gate * (pre * sig)).astype(BF16)
    slope_ref[...] = gate * (sig * (1.0 + pre * (1.0 - sig)))


def slope_kernel(n, me_ref, slope_ref, *refs):
    ys, (w_ref, grad_ref) = refs[:n], refs[n:]
    width = ys[0].shape[1]
    grad = sum(
        dot(ys[s][...], w_ref[:, place(me_ref, s, width)], ((1,), (1,))) for s in range(n)
    )
    grad_ref[...] = (grad * slope_ref[...]).astype(BF16)


def mix_kernel(me_ref, act_ref, w_ref, out_ref):
    out_ref[0] = dot(act_ref[...], w_ref[...]).astype(BF16)


def back_kernel(me_ref, grad_ref, w_ref, out_ref):
    hid = w_ref.shape[2]
    total = sum(
        dot(grad_ref[:, e * hid : (e + 1) * hid], w_ref[e], ((1,), (1,)))
        for e in range(w_ref.shape[0])
    )
    out_ref[0] = total.astype(BF16)


def d_out_kernel(n, me_ref, act_ref, *refs):
    ys, out_ref = refs[:n], refs[n]
    width = ys[0].shape[1]
    act = act_ref[...].T
    for s in range(n):
        out_ref[:, place(me_ref, s, width)] = dot(act, ys[s][...]).astype(BF16)


def d_in_kernel(n, me_ref, grad_ref, *refs):
    xs, out_ref = refs[:n], refs[n]
    width = xs[0].shape[0]
    grad = grad_ref[...]
    for s in range(n):
        out_ref[0, place(me_ref, s, width), :] = dot(xs[s][...], grad).astype(BF16)


def call(kernel, name, grid, in_specs, out_specs, out_shape, args, flops):
    moved = sum(a.size * a.dtype.itemsize for a in args)
    moved += sum(o.size * o.dtype.itemsize for o in jax.tree.leaves(out_shape))
    return pl.pallas_call(
        kernel,
        grid_spec=pltpu.PrefetchScalarGridSpec(
            num_scalar_prefetch=1, grid=grid, in_specs=in_specs, out_specs=out_specs
        ),
        out_shape=out_shape,
        name=name,
        cost_estimate=pl.CostEstimate(flops=flops, bytes_accessed=moved, transcendentals=0),
        compiler_params=pltpu.CompilerParams(vmem_limit_bytes=LIMIT),
    )(*args)


def once(shape, index):
    return pl.BlockSpec(shape, index, pipeline_mode=pl.Buffered(1))


def shards(tokens, cotangent, routing, gates, w_in, w_out):
    n = lax.axis_size("tensor")
    local, width, hid = w_in.shape
    rows, quarter = tokens.shape
    me = lax.axis_index("tensor").astype(jnp.int32).reshape(1)

    routed = jnp.concatenate([routing.astype(F32), gates], axis=1)
    own_x = gather_rows(tokens)
    routed = gather_rows(routed)
    xs = gather_chunks(own_x)
    own_y = gather_rows(cotangent)
    ys = gather_chunks(own_y)
    total = own_x.shape[0]
    top = routing.shape[1]
    first = lax.axis_index("expert") * local
    experts = (first + jnp.arange(local, dtype=jnp.int32)).astype(F32)
    match = routed[:, :top, None] == experts[None, None, :]
    gate = jnp.sum(jnp.where(match, routed[:, top:, None], 0.0), axis=1)

    tile = min(total, 256)
    tiles = total // tile
    cols = min(512, quarter)
    per = quarter // cols
    flat_out = w_out.reshape(local * hid, width)
    flops = 2 * total * local * hid * width
    flat = jax.ShapeDtypeStruct((total, local * hid), BF16)

    x_specs = [once((tile, quarter), lambda e, t, me: (t, 0))] * n
    act, slope = call(
        functools.partial(preact_kernel, n),
        "preact",
        (local, tiles),
        [pl.BlockSpec((tile, local), lambda e, t, me: (t, 0))]
        + x_specs
        + [pl.BlockSpec((1, width, hid), lambda e, t, me: (e, 0, 0))],
        [pl.BlockSpec((tile, hid), lambda e, t, me: (t, e))] * 2,
        [flat, jax.ShapeDtypeStruct(flat.shape, F32)],
        (me, gate, *xs, w_in),
        flops,
    )

    def parts(kernel, name, left, weights, odd):
        is_out = weights.ndim == 2

        def w_index(i, j, t, me):
            block = (me[0] ^ (2 * i + odd)) * per + j
            return (0, block) if is_out else (0, block, 0)

        w_block = (local * hid, cols) if is_out else (local, cols, hid)
        return call(
            kernel,
            name,
            (n // 2, per, tiles),
            [
                pl.BlockSpec((tile, local * hid), lambda i, j, t, me: (t, 0)),
                pl.BlockSpec(w_block, w_index),
            ],
            pl.BlockSpec((1, tile, cols), lambda i, j, t, me: (i, t, j)),
            jax.ShapeDtypeStruct((n // 2, total, quarter), BF16),
            (me, left, weights),
            flops // 2,
        )

    mix_odd = parts(mix_kernel, "mix_odd", act, flat_out, 1)
    mix_even = parts(mix_kernel, "mix_even", act, flat_out, 0)
    mixed = scatter_rows(scatter_chunks(mix_even, mix_odd), rows).astype(BF16)

    grad = call(
        functools.partial(slope_kernel, n),
        "grad_preact",
        (local, tiles),
        [pl.BlockSpec((tile, hid), lambda e, t, me: (t, e))]
        + x_specs
        + [pl.BlockSpec((hid, width), lambda e, t, me: (e, 0))],
        pl.BlockSpec((tile, hid), lambda e, t, me: (t, e)),
        flat,
        (me, slope, *ys, flat_out),
        flops,
    )

    back_odd = parts(back_kernel, "back_odd", grad, w_in, 1)
    back_even = parts(back_kernel, "back_even", grad, w_in, 0)
    d_tokens = scatter_rows(scatter_chunks(back_even, back_odd), rows).astype(BF16)

    d_w_out = call(
        functools.partial(d_out_kernel, n),
        "d_w_out",
        (local,),
        [pl.BlockSpec((total, hid), lambda e, me: (0, e))]
        + [once((total, quarter), lambda e, me: (0, 0))] * n,
        pl.BlockSpec((hid, width), lambda e, me: (e, 0)),
        jax.ShapeDtypeStruct((local * hid, width), BF16),
        (me, act, *ys),
        flops,
    ).reshape(w_out.shape)
    d_w_in = call(
        functools.partial(d_in_kernel, n),
        "d_w_in",
        (local,),
        [pl.BlockSpec((total, hid), lambda e, me: (0, e))]
        + [once((quarter, total), lambda e, me: (0, 0))] * n,
        pl.BlockSpec((1, width, hid), lambda e, me: (e, 0, 0)),
        jax.ShapeDtypeStruct(w_in.shape, BF16),
        (me, grad, *[x.T for x in xs]),
        flops,
    )
    return mixed, d_tokens, d_w_in, d_w_out


def solution(mesh):
    rows = P("expert", "tensor")
    routes = P("expert", None)
    columns_in = P("expert", None, "tensor")
    rows_out = P("expert", "tensor", None)
    return jax.shard_map(
        shards,
        mesh=mesh,
        in_specs=(rows, rows, routes, routes, columns_in, rows_out),
        out_specs=(rows, rows, columns_in, rows_out),
        check_vma=False,
    )
```

```python
import functools

import jax
import jax.numpy as jnp
from jax import lax
from jax.experimental import pallas as pl
from jax.experimental.pallas import tpu as pltpu
from jax.sharding import PartitionSpec as P

MIB = 1024 * 1024
F32 = jnp.float32
BF16 = jnp.bfloat16


def swap(value, axis, bits):
    size = lax.axis_size(axis)
    return lax.ppermute(value, axis, [(i, i ^ bits) for i in range(size)])


def gather_all(value):
    shape = (lax.axis_size("expert"), lax.axis_size("tensor"), *value.shape)
    return lax.all_gather(value, ("expert", "tensor"), axis=0, tiled=False).reshape(shape)


def scatter_rows(value, rows):
    blocks = value.reshape(-1, rows, value.shape[1])
    blocks = lax.all_to_all(blocks, "expert", split_axis=0, concat_axis=0, tiled=True)
    return jnp.sum(blocks.astype(F32), axis=0)


def scatter_chunks(even, odd):
    size = lax.axis_size("tensor")
    got = swap(odd, "tensor", 1)
    parts = [even[i].astype(F32) + got[i].astype(F32) for i in range(size // 2)]
    bit = 2
    while bit < size:
        kept = []
        for i in range(len(parts) // 2):
            sent = parts[2 * i + 1].astype(BF16)
            kept.append(parts[2 * i] + swap(sent, "tensor", bit).astype(F32))
        parts = kept
        bit *= 2
    return parts[0].astype(BF16)


def column(gates, index):
    lane = lax.broadcasted_iota(jnp.int32, gates.shape, 1)
    return jnp.sum(jnp.where(lane == index, gates, 0.0), axis=1, keepdims=True)


def dot(a, b, dims=((1,), (0,))):
    return lax.dot_general(a, b, (dims, ((), ())), preferred_element_type=F32)


def chunk(ref, c):
    part = ref[:, c]
    return part.reshape(part.shape[0] * part.shape[1], part.shape[2])


def preact_kernel(me_ref, gates_ref, x_ref, *refs):
    ws, (act_ref, slope_ref) = refs[:-2], refs[-2:]
    pre = sum(dot(chunk(x_ref, c), w[0]) for c, w in enumerate(ws))
    sig = jax.nn.sigmoid(pre)
    gate = column(gates_ref[...], pl.program_id(0))
    act_ref[...] = (gate * (pre * sig)).astype(BF16)
    slope_ref[...] = gate * (sig * (1.0 + pre * (1.0 - sig)))


def slope_kernel(me_ref, slope_ref, y_ref, *refs):
    ws, grad_ref = refs[:-1], refs[-1]
    grad = sum(dot(chunk(y_ref, c), w[...], ((1,), (1,))) for c, w in enumerate(ws))
    grad_ref[...] = (grad * slope_ref[...]).astype(BF16)


def mix_kernel(me_ref, act_ref, *refs):
    ws, out_ref = refs[:-1], refs[-1]
    deep = ws[0].shape[0]
    total = sum(dot(act_ref[:, q * deep : (q + 1) * deep], w[...]) for q, w in enumerate(ws))
    out_ref[0] = total.astype(BF16)


def back_kernel(me_ref, grad_ref, *refs):
    ws, out_ref = refs[:-1], refs[-1]
    group, _, hid = ws[0].shape
    total = 0.0
    for q, w in enumerate(ws):
        for i in range(group):
            e = q * group + i
            total = total + dot(grad_ref[:, e * hid : (e + 1) * hid], w[i], ((1,), (1,)))
    out_ref[0] = total.astype(BF16)


def write_out(step, steps, slot, c, value, out, buffer, sems):
    copy = pltpu.make_async_copy(buffer.at[slot, c], out, sems.at[slot, c])

    @pl.when(step >= 2)
    def _():
        copy.wait()

    buffer[slot, c] = value().astype(BF16)
    copy.start()


def drain(step, steps, out, buffer, sems):
    @pl.when(step == steps - 1)
    def _():
        for slot in range(min(2, steps)):
            for c in range(buffer.shape[1]):
                pltpu.make_async_copy(buffer.at[slot, c], out, sems.at[slot, c]).wait()


def d_out_kernel(steps, me_ref, act_ref, y_ref, out_ref, buffer, sems):
    e = pl.program_id(0)
    _, n, hid, width = buffer.shape
    act = act_ref[...].T
    rows = pl.ds(pl.multiple_of(e * hid, hid), hid)
    for c in range(n):
        out = out_ref.at[rows, pl.ds(c * width, width)]
        write_out(e, steps, e % 2, c, lambda: dot(act, chunk(y_ref, c)), out, buffer, sems)
    drain(e, steps, out_ref.at[rows, pl.ds(0, width)], buffer, sems)


def d_in_kernel(steps, me_ref, grad_ref, x_ref, out_ref, flipped, buffer, sems):
    e = pl.program_id(0)
    _, n, width, hid = buffer.shape

    @pl.when(e == 0)
    def _():
        for c in range(n):
            flipped[c] = chunk(x_ref, c).T

    grad = grad_ref[...]
    for c in range(n):
        out = out_ref.at[e, pl.ds(c * width, width), :]
        write_out(e, steps, e % 2, c, lambda: dot(flipped[c], grad), out, buffer, sems)
    drain(e, steps, out_ref.at[e, pl.ds(0, width), :], buffer, sems)


def call(kernel, name, grid, in_specs, out_specs, out_shape, args, flops, limit, scratch=()):
    moved = sum(a.size * a.dtype.itemsize for a in {id(a): a for a in args}.values())
    moved += sum(o.size * o.dtype.itemsize for o in jax.tree.leaves(out_shape))
    return pl.pallas_call(
        kernel,
        grid_spec=pltpu.PrefetchScalarGridSpec(
            num_scalar_prefetch=1,
            grid=grid,
            in_specs=in_specs,
            out_specs=out_specs,
            scratch_shapes=scratch,
        ),
        out_shape=out_shape,
        name=name,
        cost_estimate=pl.CostEstimate(flops=flops, bytes_accessed=moved, transcendentals=0),
        compiler_params=pltpu.CompilerParams(vmem_limit_bytes=limit),
    )(*args)


def once(shape, index):
    return pl.BlockSpec(shape, index, pipeline_mode=pl.Buffered(1))


def shards(tokens, cotangent, routing, gates, w_in, w_out):
    n = lax.axis_size("tensor")
    groups = lax.axis_size("expert")
    local, width, hid = w_in.shape
    rows, quarter = tokens.shape
    total = groups * rows
    top = routing.shape[1]
    me = lax.axis_index("tensor").astype(jnp.int32).reshape(1)

    xs = gather_all(tokens)
    routed = jnp.concatenate([routing.astype(F32), gates], axis=1)
    routed = lax.all_gather(routed, "expert", axis=0, tiled=True)
    ys = gather_all(cotangent)
    first = lax.axis_index("expert") * local
    experts = (first + jnp.arange(local, dtype=jnp.int32)).astype(F32)
    match = routed[:, :top, None] == experts[None, None, :]
    gate = jnp.sum(jnp.where(match, routed[:, top:, None], 0.0), axis=1)

    held = min(groups, max(1, 256 // rows))
    tile = held * rows
    tiles = groups // held
    limit = (32 if tiles == 1 else 56) * MIB
    cols = min(512, quarter)
    per = quarter // cols
    flat_out = w_out.reshape(local * hid, width)
    flops = 2 * total * local * hid * width
    flat = jax.ShapeDtypeStruct((total, local * hid), BF16)
    streams = min(4, local)

    x_spec = once((held, n, rows, quarter), lambda e, t, me: (t, 0, 0, 0))
    act, slope = call(
        preact_kernel,
        "preact",
        (local, tiles),
        [pl.BlockSpec((tile, local), lambda e, t, me: (t, 0)), x_spec]
        + [
            pl.BlockSpec((1, quarter, hid), lambda e, t, me, c=c: (e, c, 0))
            for c in range(n)
        ],
        [pl.BlockSpec((tile, hid), lambda e, t, me: (t, e))] * 2,
        [flat, jax.ShapeDtypeStruct(flat.shape, F32)],
        (me, gate, xs, *[w_in] * n),
        flops,
        limit,
    )

    def parts(kernel, name, left, weights, odd):
        is_out = weights.ndim == 2

        def w_spec(q):
            def index(i, j, t, me):
                block = (me[0] ^ (2 * i + odd)) * per + j
                return (q, block) if is_out else (q, block, 0)

            shape = (local * hid // streams, cols) if is_out else (local // streams, cols, hid)
            return pl.BlockSpec(shape, index)

        return call(
            kernel,
            name,
            (n // 2, per, tiles),
            [pl.BlockSpec((tile, local * hid), lambda i, j, t, me: (t, 0))]
            + [w_spec(q) for q in range(streams)],
            pl.BlockSpec((1, tile, cols), lambda i, j, t, me: (i, t, j)),
            jax.ShapeDtypeStruct((n // 2, total, quarter), BF16),
            (me, left, *[weights] * streams),
            flops // 2,
            limit,
        )

    mix_odd = parts(mix_kernel, "mix_odd", act, flat_out, 1)
    mix_even = parts(mix_kernel, "mix_even", act, flat_out, 0)
    mixed = scatter_rows(scatter_chunks(mix_even, mix_odd), rows).astype(BF16)

    grad = call(
        slope_kernel,
        "grad_preact",
        (local, tiles),
        [pl.BlockSpec((tile, hid), lambda e, t, me: (t, e)), x_spec]
        + [pl.BlockSpec((hid, quarter), lambda e, t, me, c=c: (e, c)) for c in range(n)],
        pl.BlockSpec((tile, hid), lambda e, t, me: (t, e)),
        flat,
        (me, slope, ys, *[flat_out] * n),
        flops,
        limit,
    )

    back_odd = parts(back_kernel, "back_odd", grad, w_in, 1)
    back_even = parts(back_kernel, "back_even", grad, w_in, 0)
    d_tokens = scatter_rows(scatter_chunks(back_even, back_odd), rows).astype(BF16)

    whole_spec = once((groups, n, rows, quarter), lambda e, me: (0, 0, 0, 0))
    row_spec = pl.BlockSpec((total, hid), lambda e, me: (0, e))
    anywhere = pl.BlockSpec(memory_space=pl.ANY)
    sems = pltpu.SemaphoreType.DMA((2, n))
    d_w_out = call(
        functools.partial(d_out_kernel, local),
        "d_w_out",
        (local,),
        [row_spec, whole_spec],
        anywhere,
        jax.ShapeDtypeStruct((local * hid, width), BF16),
        (me, act, ys),
        flops,
        limit,
        [pltpu.VMEM((2, n, hid, quarter), BF16), sems],
    ).reshape(w_out.shape)
    d_w_in = call(
        functools.partial(d_in_kernel, local),
        "d_w_in",
        (local,),
        [row_spec, whole_spec],
        anywhere,
        jax.ShapeDtypeStruct(w_in.shape, BF16),
        (me, grad, xs),
        flops,
        limit,
        [
            pltpu.VMEM((n, quarter, total), BF16),
            pltpu.VMEM((2, n, quarter, hid), BF16),
            sems,
        ],
    )
    return mixed, d_tokens, d_w_in, d_w_out


def solution(mesh):
    rows = P("expert", "tensor")
    routes = P("expert", None)
    columns_in = P("expert", None, "tensor")
    rows_out = P("expert", "tensor", None)
    return jax.shard_map(
        shards,
        mesh=mesh,
        in_specs=(rows, rows, routes, routes, columns_in, rows_out),
        out_specs=(rows, rows, columns_in, rows_out),
        check_vma=False,
    )
```

```python
import functools

import jax
import jax.numpy as jnp
from jax import lax
from jax.experimental import pallas as pl
from jax.experimental.pallas import tpu as pltpu
from jax.sharding import PartitionSpec as P

MIB = 1024 * 1024
DEPTH = 3
F32 = jnp.float32
BF16 = jnp.bfloat16
ANYWHERE = pl.BlockSpec(memory_space=pl.ANY)


def swap(value, axis, bits):
    size = lax.axis_size(axis)
    return lax.ppermute(value, axis, [(i, i ^ bits) for i in range(size)])


def gather_rows(value):
    copies = jnp.broadcast_to(value[None], (lax.axis_size("expert"), *value.shape))
    return lax.all_to_all(copies, "expert", split_axis=0, concat_axis=0, tiled=True)


def gather_chunks(value):
    chunks = {0: value}
    bit = lax.axis_size("tensor") // 2
    while bit:
        chunks.update({s | bit: swap(c, "tensor", bit) for s, c in list(chunks.items())})
        bit //= 2
    return [chunks[s] for s in range(len(chunks))]


def scatter_rows(value, rows):
    blocks = value.reshape(-1, rows, value.shape[1])
    blocks = lax.all_to_all(blocks, "expert", split_axis=0, concat_axis=0, tiled=True)
    return jnp.sum(blocks.astype(F32), axis=0)


def scatter_chunks(even, odd):
    size = lax.axis_size("tensor")
    got = swap(odd, "tensor", 1)
    parts = [even[i].astype(F32) + got[i].astype(F32) for i in range(size // 2)]
    bit, passed = 2, ()
    while bit < size:
        kept = []
        for i in range(len(parts) // 2):
            sent = parts[2 * i + 1].astype(BF16)
            passed = passed or (sent,)
            kept.append(parts[2 * i] + swap(sent, "tensor", bit).astype(F32))
        parts = kept
        bit *= 2
    return parts[0].astype(BF16), passed


def pack_routes(routing, gates, lanes=128):
    high = lax.reduce_precision(gates, 8, 7)
    middle = lax.reduce_precision(gates - high, 8, 7)
    low = gates - high - middle
    packed = jnp.concatenate([routing.astype(F32), high, middle, low], axis=1)
    return jnp.pad(packed, ((0, 0), (0, lanes - packed.shape[1]))).astype(BF16)


def unpack_gates(packed, top, first, local):
    packed = packed[:, : 4 * top].astype(F32)
    chosen, high, middle, low = (packed[:, i * top : (i + 1) * top] for i in range(4))
    value = high + middle + low
    experts = (first + jnp.arange(local, dtype=jnp.int32)).astype(F32)
    match = chosen[:, :, None] == experts[None, None, :]
    return jnp.sum(jnp.where(match, value[:, :, None], 0.0), axis=1)


def column(gates, index):
    lane = lax.broadcasted_iota(jnp.int32, gates.shape, 1)
    return jnp.sum(jnp.where(lane == index, gates, 0.0), axis=1, keepdims=True)


def dot(a, b, dims=((1,), (0,))):
    return lax.dot_general(a, b, (dims, ((), ())), preferred_element_type=F32)


def flat_rows(part):
    return part.reshape(part.shape[0] * part.shape[1], part.shape[2])


def stream(copies, step, steps, first):
    @pl.when(first & (step == 0))
    def _():
        for ahead in range(min(DEPTH - 1, steps)):
            for copy in copies(ahead):
                copy.start()

    @pl.when(first & (step + DEPTH - 1 < steps))
    def _():
        for copy in copies(step + DEPTH - 1):
            copy.start()

    @pl.when(first)
    def _():
        for copy in copies(step):
            copy.wait()


def block(index, size):
    return pl.ds(pl.multiple_of(index * size, size), size)


def preact_kernel(pieces, steps, me_ref, gates_ref, *refs):
    xs, (w_ref, act_ref, slope_ref, buffer, sems) = refs[: len(pieces)], refs[-5:]
    e = pl.program_id(0)
    _, n, width, hid = buffer.shape

    def copies(step):
        slot = step % DEPTH
        return [
            pltpu.make_async_copy(
                w_ref.at[step, block(me_ref[0] ^ s, width), :], buffer.at[slot, s], sems.at[slot, s]
            )
            for s in range(n)
        ]

    stream(copies, e, steps, pl.program_id(1) == 0)
    pre = 0.0
    for x, (s, start) in zip(xs, pieces):
        w = buffer[e % DEPTH, s, start : start + x.shape[2], :]
        pre = pre + dot(flat_rows(x[...]), w)
    sig = jax.nn.sigmoid(pre)
    gate = column(gates_ref[...], e)
    act_ref[...] = (gate * (pre * sig)).astype(BF16)
    slope_ref[...] = gate * (sig * (1.0 + pre * (1.0 - sig)))


def slope_kernel(pieces, steps, me_ref, slope_ref, *refs):
    ys, w_ref, (grad_ref, buffer, sems) = refs[: len(pieces)], refs[len(pieces)], refs[-3:]
    e = pl.program_id(0)
    _, n, hid, width = buffer.shape

    def copies(step):
        slot = step % DEPTH
        return [
            pltpu.make_async_copy(
                w_ref.at[block(step, hid), block(me_ref[0] ^ s, width)],
                buffer.at[slot, s],
                sems.at[slot, s],
            )
            for s in range(n)
        ]

    stream(copies, e, steps, pl.program_id(1) == 0)
    grad = 0.0
    for y, (s, start) in zip(ys, pieces):
        w = buffer[e % DEPTH, s, :, start : start + y.shape[2]]
        grad = grad + dot(flat_rows(y[...]), w, ((1,), (1,)))
    grad_ref[...] = (grad * slope_ref[...]).astype(BF16)


def mix_kernel(steps, per, odd, me_ref, act_ref, w_ref, *refs):
    out_ref, buffer, sems = refs[-3:]
    _, pieces, deep, cols = buffer.shape
    step = pl.program_id(0)

    def copies(step):
        slot = step % DEPTH
        column_block = (me_ref[0] ^ (2 * (step // per) + odd)) * per + step % per
        return [
            pltpu.make_async_copy(
                w_ref.at[pl.ds(q * deep, deep), block(column_block, cols)],
                buffer.at[slot, q],
                sems.at[slot, q],
            )
            for q in range(pieces)
        ]

    stream(copies, step, steps, pl.program_id(1) == 0)
    weights = buffer[step % DEPTH].reshape(pieces * deep, cols)
    out_ref[0] = dot(act_ref[...], weights).astype(BF16)


def back_kernel(steps, per, odd, me_ref, grad_ref, w_ref, *refs):
    out_ref, buffer, sems = refs[-3:]
    _, pieces, group, cols, hid = buffer.shape
    step = pl.program_id(0)

    def copies(step):
        slot = step % DEPTH
        column_block = (me_ref[0] ^ (2 * (step // per) + odd)) * per + step % per
        return [
            pltpu.make_async_copy(
                w_ref.at[pl.ds(q * group, group), block(column_block, cols), :],
                buffer.at[slot, q],
                sems.at[slot, q],
            )
            for q in range(pieces)
        ]

    stream(copies, step, steps, pl.program_id(1) == 0)
    total = 0.0
    for e in range(pieces * group):
        w = buffer[step % DEPTH, e // group, e % group]
        total = total + dot(grad_ref[:, e * hid : (e + 1) * hid], w, ((1,), (1,)))
    out_ref[0] = total.astype(BF16)


def drain(step, steps, out, buffer, sems):
    @pl.when(step == steps - 1)
    def _():
        for slot in range(min(2, steps)):
            for s in range(buffer.shape[1]):
                pltpu.make_async_copy(buffer.at[slot, s], out, sems.at[slot, s]).wait()


def write_step(step, steps, values, outs, buffer, sems):
    slot = step % 2

    @pl.when(step >= 2)
    def _():
        for s, out in enumerate(outs):
            pltpu.make_async_copy(buffer.at[slot, s], out, sems.at[slot, s]).wait()

    for s, value in enumerate(values()):
        buffer[slot, s] = value.astype(BF16)
    for s, out in enumerate(outs):
        pltpu.make_async_copy(buffer.at[slot, s], out, sems.at[slot, s]).start()
    drain(step, steps, outs[0], buffer, sems)


def d_out_kernel(pieces, steps, me_ref, act_ref, *refs):
    ys, (out_ref, buffer, sems) = refs[: len(pieces)], refs[-3:]
    e = pl.program_id(0)
    _, n, hid, width = buffer.shape
    act = act_ref[...].T
    outs = [out_ref.at[block(e, hid), block(me_ref[0] ^ s, width)] for s in range(n)]

    def values():
        for s in range(n):
            yield dot(act, flat_rows(ys[s][...]))

    write_step(e, steps, values, outs, buffer, sems)


def d_in_kernel(pieces, steps, me_ref, grad_ref, *refs):
    xs, (out_ref, flipped, buffer, sems) = refs[: len(pieces)], refs[-4:]
    e = pl.program_id(0)
    _, n, width, hid = buffer.shape

    @pl.when(e == 0)
    def _():
        for x, (s, start) in zip(xs, pieces):
            flipped[s, start : start + x.shape[2], :] = flat_rows(x[...]).T

    grad = grad_ref[...]
    outs = [out_ref.at[e, block(me_ref[0] ^ s, width), :] for s in range(n)]

    def values():
        for s in range(n):
            yield dot(flipped[s], grad)

    write_step(e, steps, values, outs, buffer, sems)


def call(kernel, name, grid, in_specs, out_specs, out_shape, args, flops, limit, scratch, after=()):
    moved = sum(a.size * a.dtype.itemsize for a in args)
    moved += sum(o.size * o.dtype.itemsize for o in jax.tree.leaves(out_shape))
    return pl.pallas_call(
        kernel,
        grid_spec=pltpu.PrefetchScalarGridSpec(
            num_scalar_prefetch=1,
            grid=grid,
            in_specs=in_specs + [ANYWHERE] * len(after),
            out_specs=out_specs,
            scratch_shapes=scratch,
        ),
        out_shape=out_shape,
        name=name,
        cost_estimate=pl.CostEstimate(flops=flops, bytes_accessed=moved, transcendentals=0),
        compiler_params=pltpu.CompilerParams(vmem_limit_bytes=limit),
    )(*args, *after)


def once(shape, index):
    return pl.BlockSpec(shape, index, pipeline_mode=pl.Buffered(1))


def shards(tokens, cotangent, routing, gates, w_in, w_out):
    n = lax.axis_size("tensor")
    groups = lax.axis_size("expert")
    local, width, hid = w_in.shape
    rows, quarter = tokens.shape
    half = quarter // 2
    total = groups * rows
    top = routing.shape[1]
    me = lax.axis_index("tensor").astype(jnp.int32).reshape(1)

    packed = jnp.concatenate([tokens[:, :half], pack_routes(routing, gates)], axis=1)
    left = gather_rows(packed)
    right = gather_rows(tokens[:, half:])
    whole = gather_rows(cotangent)
    lefts, rights = gather_chunks(left), gather_chunks(right)
    ys = gather_chunks(whole)
    xs = lefts + rights
    x_pieces = [(s, 0) for s in range(n)] + [(s, half) for s in range(n)]
    y_pieces = [(s, 0) for s in range(n)]
    x_widths, y_widths = [half] * (2 * n), [quarter] * n
    first = lax.axis_index("expert") * local
    gate = unpack_gates(left[:, :, half:].reshape(total, -1), top, first, local)

    held = min(groups, max(1, 256 // rows))
    tile = held * rows
    tiles = groups // held
    limit = (32 if tiles == 1 else 56) * MIB
    cols = min(512, quarter)
    per = quarter // cols
    flat_out = w_out.reshape(local * hid, width)
    flops = 2 * total * local * hid * width
    flat = jax.ShapeDtypeStruct((total, local * hid), BF16)
    streams = min(4, local)

    def tile_specs(widths):
        return [once((held, rows, w), lambda e, t, me: (t, 0, 0)) for w in widths]

    def ring(*shape):
        return [
            pltpu.VMEM((DEPTH, *shape), BF16),
            pltpu.SemaphoreType.DMA((DEPTH, shape[0])),
        ]

    act, slope = call(
        functools.partial(preact_kernel, x_pieces, local),
        "preact",
        (local, tiles),
        [pl.BlockSpec((tile, local), lambda e, t, me: (t, 0))] + tile_specs(x_widths) + [ANYWHERE],
        [pl.BlockSpec((tile, hid), lambda e, t, me: (t, e))] * 2,
        [flat, jax.ShapeDtypeStruct(flat.shape, F32)],
        (me, gate, *xs, w_in),
        flops,
        limit,
        ring(n, quarter, hid),
    )

    def parts(kernel, name, left, weights, odd, after=()):
        if weights.ndim == 2:
            shape = (streams, local * hid // streams, cols)
        else:
            shape = (streams, local // streams, cols, hid)
        steps = n // 2 * per
        return call(
            functools.partial(kernel, steps, per, odd),
            name,
            (steps, tiles),
            [pl.BlockSpec((tile, local * hid), lambda i, t, me: (t, 0)), ANYWHERE],
            pl.BlockSpec((1, tile, cols), lambda i, t, me: (i // per, t, i % per)),
            jax.ShapeDtypeStruct((n // 2, total, quarter), BF16),
            (me, left, weights),
            flops // 2,
            limit,
            ring(*shape),
            after,
        )

    mix_odd = parts(mix_kernel, "mix_odd", act, flat_out, 1)
    mix_even = parts(mix_kernel, "mix_even", act, flat_out, 0, (mix_odd,))
    mix_sum, mix_passed = scatter_chunks(mix_even, mix_odd)
    mixed = scatter_rows(mix_sum, rows).astype(BF16)

    grad = call(
        functools.partial(slope_kernel, y_pieces, local),
        "grad_preact",
        (local, tiles),
        [pl.BlockSpec((tile, hid), lambda e, t, me: (t, e))] + tile_specs(y_widths) + [ANYWHERE],
        pl.BlockSpec((tile, hid), lambda e, t, me: (t, e)),
        flat,
        (me, slope, *ys, flat_out),
        flops,
        limit,
        ring(n, hid, quarter),
        mix_passed,
    )

    back_odd = parts(back_kernel, "back_odd", grad, w_in, 1, (mix_sum,))
    back_even = parts(back_kernel, "back_even", grad, w_in, 0, (back_odd,))
    back_sum, back_passed = scatter_chunks(back_even, back_odd)
    d_tokens = scatter_rows(back_sum, rows).astype(BF16)

    def whole_specs(widths):
        return [once((groups, rows, w), lambda e, me: (0, 0, 0)) for w in widths]

    row_spec = pl.BlockSpec((total, hid), lambda e, me: (0, e))
    sems = pltpu.SemaphoreType.DMA((2, n))
    d_w_out = call(
        functools.partial(d_out_kernel, y_pieces, local),
        "d_w_out",
        (local,),
        [row_spec] + whole_specs(y_widths),
        ANYWHERE,
        jax.ShapeDtypeStruct((local * hid, width), BF16),
        (me, act, *ys),
        flops,
        limit,
        [pltpu.VMEM((2, n, hid, quarter), BF16), sems],
        back_passed,
    )
    d_w_in = call(
        functools.partial(d_in_kernel, x_pieces, local),
        "d_w_in",
        (local,),
        [row_spec] + whole_specs(x_widths),
        ANYWHERE,
        jax.ShapeDtypeStruct(w_in.shape, BF16),
        (me, grad, *xs),
        flops,
        limit,
        [
            pltpu.VMEM((n, quarter, total), BF16),
            pltpu.VMEM((2, n, quarter, hid), BF16),
            sems,
        ],
        (d_w_out, back_sum),
    )
    return mixed, d_tokens, d_w_in, d_w_out.reshape(w_out.shape)


def solution(mesh):
    rows = P("expert", "tensor")
    routes = P("expert", None)
    columns_in = P("expert", None, "tensor")
    rows_out = P("expert", "tensor", None)
    return jax.shard_map(
        shards,
        mesh=mesh,
        in_specs=(rows, rows, routes, routes, columns_in, rows_out),
        out_specs=(rows, rows, columns_in, rows_out),
        check_vma=False,
    )
```

```python
import functools
import math

import jax
import jax.numpy as jnp
from jax import lax
from jax.experimental import pallas as pl
from jax.experimental.pallas import tpu as pltpu
from jax.sharding import PartitionSpec as P

MIB = 1024 * 1024
LANES = 128
F32 = jnp.float32
BF16 = jnp.bfloat16
EXACT = lax.Precision.HIGHEST
ANYWHERE = pl.BlockSpec(memory_space=pl.ANY)
DEPTH = 3


def swap(value, axis, bits):
    size = lax.axis_size(axis)
    return lax.ppermute(value, axis, [(i, i ^ bits) for i in range(size)])


def exchange_rows(blocks):
    return lax.all_to_all(blocks, "expert", split_axis=0, concat_axis=0, tiled=True)


def gather_chunks(value):
    chunks = {0: value}
    bit = lax.axis_size("tensor") // 2
    while bit:
        chunks.update({s | bit: swap(c, "tensor", bit) for s, c in list(chunks.items())})
        bit //= 2
    return [chunks[s] for s in range(len(chunks))]


def scatter_rows(value, rows):
    return jnp.sum(exchange_rows(value.reshape(-1, rows, value.shape[1])).astype(F32), axis=0)


def scatter_chunks(even, odd):
    size = lax.axis_size("tensor")
    got = swap(odd, "tensor", 1)
    parts = [even[i].astype(F32) + got[i].astype(F32) for i in range(size // 2)]
    bit, passed = 2, ()
    while bit < size:
        kept = []
        for i in range(len(parts) // 2):
            sent = parts[2 * i + 1].astype(BF16)
            passed = passed or (sent,)
            kept.append(parts[2 * i] + swap(sent, "tensor", bit).astype(F32))
        parts = kept
        bit *= 2
    return parts[0].astype(BF16), passed


def dot(a, b, dims=((1,), (0,)), precision=None):
    return lax.dot_general(
        a, b, (dims, ((), ())), precision=precision, preferred_element_type=F32
    )


def iota(shape, dim):
    return lax.broadcasted_iota(jnp.int32, shape, dim)


def flat_rows(part):
    return part.reshape(part.shape[0] * part.shape[1], part.shape[2])


def block(index, size):
    return pl.ds(pl.multiple_of(index * size, size), size)


def placed(space, shape, dtype=BF16):
    return space(shape, dtype)


def stream(copies, step, steps):
    @pl.when(step == 0)
    def _():
        for ahead in range(min(DEPTH - 1, steps)):
            for copy in copies(ahead):
                copy.start()

    @pl.when(step + DEPTH - 1 < steps)
    def _():
        for copy in copies(step + DEPTH - 1):
            copy.start()


def gather(to_row_ref, sources, held_ref, rows_ref, sems):
    copies = [
        pltpu.make_async_copy(
            source.at[:, :, pl.ds(0, held_ref.shape[3])], held_ref.at[s], sems.at[s]
        )
        for s, source in enumerate(sources)
    ]
    for copy in copies:
        copy.start()
    for s, copy in enumerate(copies):
        copy.wait()
        rows_ref[s] = dot(to_row_ref[...], flat_rows(held_ref[s])).astype(BF16)


def pack_kernel(me_ref, token_ref, routing_ref, gates_ref, out_ref):
    _, width = token_ref.shape
    top = routing_ref.shape[1]
    gates = gates_ref[...]
    high = gates.astype(BF16)
    middle = (gates - high.astype(F32)).astype(BF16)
    low = (gates - high.astype(F32) - middle.astype(F32)).astype(BF16)
    parts = (routing_ref[...].astype(F32).astype(BF16), high, middle, low)
    lanes = (top, LANES)
    packed = sum(
        dot(part, (iota(lanes, 0) + i * top == iota(lanes, 1)).astype(F32).astype(BF16))
        for i, part in enumerate(parts)
    ).astype(BF16)
    for group in range(out_ref.shape[0]):
        out_ref[group, :, :width] = token_ref[...]
        out_ref[group, :, width:] = packed


def repeat_kernel(me_ref, token_ref, *refs):
    out_ref = refs[-1]
    for group in range(out_ref.shape[0]):
        out_ref[group] = token_ref[...]


def plan_kernel(top, local, me_ref, packed_ref, to_token_ref, to_row_ref, gate_ref):
    total, rows = to_token_ref.shape
    room = rows // local
    packed = flat_rows(packed_ref[...]).astype(F32)
    chosen = packed[:, :top]
    value = sum(packed[:, i * top : (i + 1) * top] for i in (1, 2, 3))
    lane = iota((total, local), 1)
    match = jnp.zeros((total, local), F32)
    gate = jnp.zeros((total, local), F32)
    for e in range(local):
        hit = chosen == (me_ref[1] + e).astype(F32)
        here = lane == e
        found = jnp.sum(jnp.where(hit, 1.0, 0.0), axis=1, keepdims=True)
        match = jnp.where(here, found, match)
        gate = jnp.where(here, jnp.sum(jnp.where(hit, value, 0.0), axis=1, keepdims=True), gate)
    step = min(total, 256)
    earlier = (iota((step, step), 0) > iota((step, step), 1)).astype(F32).astype(BF16)
    spread = (iota((local, rows), 1) // room == iota((local, rows), 0)).astype(F32)
    count = jnp.zeros((1, local), F32)
    gates = jnp.zeros((rows, local), F32)
    for start in range(0, total, step):
        part = match[start : start + step]
        before = dot(earlier, part.astype(BF16)) + count
        count = count + jnp.sum(part, axis=0, keepdims=True)
        place = dot(jnp.where(part > 0.0, before, -1.0), spread, precision=EXACT)
        slot = (iota((step, rows), 1) % room).astype(F32)
        one_hot = jnp.where(place == slot, 1.0, 0.0)
        to_token_ref[start : start + step, :] = one_hot.astype(BF16)
        flipped = one_hot.T
        to_row_ref[:, start : start + step] = flipped.astype(BF16)
        gates = gates + dot(flipped, gate[start : start + step], precision=EXACT)
    own = iota((rows, local), 0) // room == iota((rows, local), 1)
    gate_ref[...] = jnp.sum(jnp.where(own, gates, 0.0), axis=1, keepdims=True)


def preact_kernel(n, steps, me_ref, to_row_ref, gate_ref, *refs):
    xs, w_ref = refs[:n], refs[n]
    act_ref, spread_ref, slope_ref, held_ref, rows_ref, x_sems, buffer, sems = refs[-8:]
    room, width = act_ref.shape[0], rows_ref.shape[2]
    e = pl.program_id(0)

    def copies(step):
        slot = step % DEPTH
        return [
            pltpu.make_async_copy(
                w_ref.at[step, block(me_ref[0] ^ s, width), :], buffer.at[slot, s], sems.at[slot, s]
            )
            for s in range(n)
        ]

    stream(copies, e, steps)

    @pl.when(e == 0)
    def _():
        gather(to_row_ref, xs, held_ref, rows_ref, x_sems)

    for copy in copies(e):
        copy.wait()
    pre = sum(dot(rows_ref[s, block(e, room), :], buffer[e % DEPTH, s]) for s in range(n))
    sig = jax.nn.sigmoid(pre)
    gate = gate_ref[...]
    act = (gate * (pre * sig)).astype(BF16)
    act_ref[...] = act
    spread_ref[...] = dot(to_row_ref[block(e, room), :], act, ((0,), (0,))).astype(BF16)
    slope_ref[...] = gate * (sig * (1.0 + pre * (1.0 - sig)))


def slope_kernel(n, steps, me_ref, to_row_ref, slope_ref, *refs):
    ys, w_ref = refs[:n], refs[n]
    grad_ref, spread_ref, held_ref, rows_ref, y_sems, buffer, sems = refs[-7:]
    room, hid = grad_ref.shape
    width = rows_ref.shape[2]
    e = pl.program_id(0)

    def copies(step):
        slot = step % DEPTH
        return [
            pltpu.make_async_copy(
                w_ref.at[block(step, hid), block(me_ref[0] ^ s, width)],
                buffer.at[slot, s],
                sems.at[slot, s],
            )
            for s in range(n)
        ]

    stream(copies, e, steps)

    @pl.when(e == 0)
    def _():
        gather(to_row_ref, ys, held_ref, rows_ref, y_sems)

    for copy in copies(e):
        copy.wait()
    grad = sum(
        dot(rows_ref[s, block(e, room), :], buffer[e % DEPTH, s], ((1,), (1,))) for s in range(n)
    )
    grad = (grad * slope_ref[...]).astype(BF16)
    grad_ref[...] = grad
    spread_ref[...] = dot(to_row_ref[block(e, room), :], grad, ((0,), (0,))).astype(BF16)


def column_block(me_ref, step, per, odd):
    return (me_ref[0] ^ (2 * (step // per) + odd)) * per + step % per


def mix_kernel(steps, per, odd, me_ref, to_token_ref, act_ref, w_ref, *refs):
    out_ref, rows_ref, buffer, sems = refs[-4:]
    _, local, hid, cols = buffer.shape
    room = rows_ref.shape[0] // local
    step = pl.program_id(0)

    def copies(step):
        slot = step % DEPTH
        columns = block(column_block(me_ref, step, per, odd), cols)
        return [
            pltpu.make_async_copy(
                w_ref.at[pl.ds(e * hid, hid), columns], buffer.at[slot, e], sems.at[slot, e]
            )
            for e in range(local)
        ]

    stream(copies, step, steps)
    for copy in copies(step):
        copy.wait()
    for e in range(local):
        here = slice(e * room, (e + 1) * room)
        rows_ref[here, :] = dot(act_ref[here, :], buffer[step % DEPTH, e]).astype(BF16)
    out_ref[0] = dot(to_token_ref[...], rows_ref[...]).astype(BF16)


def back_kernel(steps, per, odd, me_ref, to_token_ref, grad_ref, w_ref, *refs):
    out_ref, rows_ref, buffer, sems = refs[-4:]
    _, local, cols, _ = buffer.shape
    room = rows_ref.shape[0] // local
    step = pl.program_id(0)

    def copies(step):
        slot = step % DEPTH
        columns = block(column_block(me_ref, step, per, odd), cols)
        return [
            pltpu.make_async_copy(
                w_ref.at[e, columns, :], buffer.at[slot, e], sems.at[slot, e]
            )
            for e in range(local)
        ]

    stream(copies, step, steps)
    for copy in copies(step):
        copy.wait()
    for e in range(local):
        here = slice(e * room, (e + 1) * room)
        part = dot(grad_ref[here, :], buffer[step % DEPTH, e], ((1,), (1,)))
        rows_ref[here, :] = part.astype(BF16)
    out_ref[0] = dot(to_token_ref[...], rows_ref[...]).astype(BF16)


def drain(step, steps, out, buffer, sems):
    @pl.when(step == steps - 1)
    def _():
        for slot in range(min(2, steps)):
            for s in range(buffer.shape[1]):
                pltpu.make_async_copy(buffer.at[slot, s], out, sems.at[slot, s]).wait()


def write_step(step, steps, values, outs, buffer, sems):
    slot = step % 2

    @pl.when(step >= 2)
    def _():
        for s, out in enumerate(outs):
            pltpu.make_async_copy(buffer.at[slot, s], out, sems.at[slot, s]).wait()

    for s, value in enumerate(values()):
        buffer[slot, s] = value.astype(BF16)
    for s, out in enumerate(outs):
        pltpu.make_async_copy(buffer.at[slot, s], out, sems.at[slot, s]).start()
    drain(step, steps, outs[0], buffer, sems)


def d_out_kernel(n, steps, me_ref, act_ref, *refs):
    ys, (out_ref, buffer, sems) = refs[:n], refs[-3:]
    e = pl.program_id(0)
    _, n, hid, width = buffer.shape
    act = act_ref[...].T
    outs = [out_ref.at[block(e, hid), block(me_ref[0] ^ s, width)] for s in range(n)]

    def values():
        for s in range(n):
            yield dot(act, flat_rows(ys[s][...]))

    write_step(e, steps, values, outs, buffer, sems)


def d_in_kernel(n, steps, me_ref, grad_ref, *refs):
    xs, (out_ref, flipped, buffer, sems) = refs[:n], refs[-4:]
    e = pl.program_id(0)
    _, n, width, hid = buffer.shape

    @pl.when(e == 0)
    def _():
        for s in range(n):
            flipped[s] = flat_rows(xs[s][...]).T

    grad = grad_ref[...]
    outs = [out_ref.at[e, block(me_ref[0] ^ s, width), :] for s in range(n)]

    def values():
        for s in range(n):
            yield dot(flipped[s], grad)

    write_step(e, steps, values, outs, buffer, sems)


def call(kernel, name, grid, in_specs, out_specs, out_shape, args, flops, limit, scratch=(), after=()):
    moved = sum(a.size * a.dtype.itemsize for a in args)
    outs = out_shape if isinstance(out_shape, list) else [out_shape]
    moved += sum(math.prod(o.shape) * jnp.dtype(o.dtype).itemsize for o in outs)
    return pl.pallas_call(
        kernel,
        grid_spec=pltpu.PrefetchScalarGridSpec(
            num_scalar_prefetch=1,
            grid=grid,
            in_specs=in_specs + [ANYWHERE] * len(after),
            out_specs=out_specs,
            scratch_shapes=scratch,
        ),
        out_shape=out_shape,
        name=name,
        cost_estimate=pl.CostEstimate(flops=flops, bytes_accessed=moved, transcendentals=0),
        compiler_params=pltpu.CompilerParams(vmem_limit_bytes=limit * MIB),
    )(*args, *after)


def once(*shape):
    return pl.BlockSpec(shape, lambda *_: (0,) * len(shape), pipeline_mode=pl.Buffered(1))


def shards(tokens, cotangent, routing, gates, w_in, w_out):
    n = lax.axis_size("tensor")
    groups = lax.axis_size("expert")
    local, width, hid = w_in.shape
    rows, quarter = tokens.shape
    total = groups * rows
    top = routing.shape[1]
    room = groups * (rows // 4)
    slots = local * room
    tensor_index = lax.axis_index("tensor").astype(jnp.int32)
    first = lax.axis_index("expert").astype(jnp.int32) * local
    me = jnp.stack([tensor_index, first])
    big = total > 256
    flops = 2 * slots * hid * width
    limit = 56 if big else 36
    dense = jax.ShapeDtypeStruct((total, local * hid), BF16)
    packed = call(
        pack_kernel,
        "pack",
        (1,),
        [once(rows, quarter), once(rows, top), once(rows, top)],
        once(groups, rows, quarter + LANES),
        jax.ShapeDtypeStruct((groups, rows, quarter + LANES), BF16),
        (me, tokens, routing, gates),
        0,
        24 if big else 4,
    )
    left = exchange_rows(packed)
    xs = gather_chunks(left)
    whole = exchange_rows(
        call(
            repeat_kernel,
            "repeat",
            (1,),
            [once(rows, quarter)],
            once(groups, rows, quarter),
            jax.ShapeDtypeStruct((groups, rows, quarter), BF16),
            (me, cotangent),
            0,
            24 if big else 4,
            (),
            (left,),
        )
    )
    ys = gather_chunks(whole)
    to_token, to_row, gate = call(
        functools.partial(plan_kernel, top, local),
        "plan",
        (1,),
        [
            pl.BlockSpec(
                (groups, rows, LANES),
                lambda i, me: (0, 0, quarter // LANES),
                pipeline_mode=pl.Buffered(1),
            )
        ],
        [once(total, slots), once(slots, total), once(slots, 1)],
        [
            jax.ShapeDtypeStruct((total, slots), BF16),
            jax.ShapeDtypeStruct((slots, total), BF16),
            jax.ShapeDtypeStruct((slots, 1), F32),
        ],
        (me, left),
        0,
        48 if big else 6,
    )

    def ring(*shape):
        return [
            pltpu.VMEM((DEPTH, *shape), BF16),
            pltpu.SemaphoreType.DMA((DEPTH, shape[0])),
        ]

    chunk_specs = [once(groups, rows, quarter)] * n
    loose = [ANYWHERE] * (n + 1)
    row_block = pl.BlockSpec((room, hid), lambda e, me: (e, 0))
    dense_block = pl.BlockSpec((total, hid), lambda e, me: (0, e))
    row_shape = jax.ShapeDtypeStruct((slots, hid), BF16)
    gathered = [
        pltpu.VMEM((n, groups, rows, quarter), BF16),
        pltpu.VMEM((n, slots, quarter), BF16),
        pltpu.SemaphoreType.DMA((n,)),
    ]
    flat_out = w_out.reshape(local * hid, width)
    act, act_dense, slope = call(
        functools.partial(preact_kernel, n, local),
        "preact",
        (local,),
        [once(slots, total), pl.BlockSpec((room, 1), lambda e, me: (e, 0))] + loose,
        [row_block, dense_block, row_block],
        [row_shape, dense, jax.ShapeDtypeStruct((slots, hid), F32)],
        (me, to_row, gate, *xs, w_in),
        flops,
        limit,
        gathered + ring(n, quarter, hid),
        (whole,),
    )
    cols = min(512, quarter)
    per = quarter // cols
    steps = n // 2 * per

    def parts(kernel, name, held, weights, odd, after=()):
        shape = (local, hid, cols) if weights.ndim == 2 else (local, cols, hid)
        return call(
            functools.partial(kernel, steps, per, odd),
            name,
            (steps,),
            [once(total, slots), once(slots, hid), ANYWHERE],
            pl.BlockSpec((1, total, cols), lambda i, me: (i // per, 0, i % per)),
            jax.ShapeDtypeStruct((n // 2, total, quarter), BF16),
            (me, to_token, held, weights),
            flops // 2,
            limit,
            [pltpu.VMEM((slots, cols), BF16)] + ring(*shape),
            after,
        )

    mix_odd = parts(mix_kernel, "mix_odd", act, flat_out, 1)
    mix_even = parts(mix_kernel, "mix_even", act, flat_out, 0, (mix_odd,))
    mix_sum, mix_passed = scatter_chunks(mix_even, mix_odd)
    mixed = scatter_rows(mix_sum, rows).astype(BF16)

    grad, grad_dense = call(
        functools.partial(slope_kernel, n, local),
        "grad_preact",
        (local,),
        [once(slots, total), row_block] + loose,
        [row_block, dense_block],
        [row_shape, dense],
        (me, to_row, slope, *ys, flat_out),
        flops,
        limit,
        gathered + ring(n, hid, quarter),
        mix_passed,
    )

    back_odd = parts(back_kernel, "back_odd", grad, w_in, 1)
    back_even = parts(back_kernel, "back_even", grad, w_in, 0, (back_odd,))
    back_sum, back_passed = scatter_chunks(back_even, back_odd)
    d_tokens = scatter_rows(back_sum, rows).astype(BF16)

    sems = pltpu.SemaphoreType.DMA((2, n))
    d_w_out = call(
        functools.partial(d_out_kernel, n, local),
        "d_w_out",
        (local,),
        [dense_block] + chunk_specs,
        pl.BlockSpec(memory_space=pltpu.HBM),
        placed(pltpu.HBM, (local * hid, width)),
        (me, act_dense, *ys),
        2 * total * local * hid * width,
        limit,
        [pltpu.VMEM((2, n, hid, quarter), BF16), sems],
        (*back_passed, mix_sum),
    )
    d_w_in = call(
        functools.partial(d_in_kernel, n, local),
        "d_w_in",
        (local,),
        [dense_block] + chunk_specs,
        pl.BlockSpec(memory_space=pltpu.HBM),
        placed(pltpu.HBM, w_in.shape),
        (me, grad_dense, *xs),
        2 * total * local * hid * width,
        limit,
        [
            pltpu.VMEM((n, quarter, total), BF16),
            pltpu.VMEM((2, n, quarter, hid), BF16),
            sems,
        ],
        (back_sum,),
    )
    return mixed, d_tokens, d_w_in, d_w_out.reshape(w_out.shape)


def solution(mesh):
    rows = P("expert", "tensor")
    routes = P("expert", None)
    columns_in = P("expert", None, "tensor")
    rows_out = P("expert", "tensor", None)
    return jax.shard_map(
        shards,
        mesh=mesh,
        in_specs=(rows, rows, routes, routes, columns_in, rows_out),
        out_specs=(rows, rows, columns_in, rows_out),
        check_vma=False,
    )
```

```python
import functools
import math

import jax
import jax.numpy as jnp
from jax import lax
from jax.experimental import pallas as pl
from jax.experimental.pallas import tpu as pltpu
from jax.sharding import PartitionSpec as P

MIB = 1024 * 1024
LANES = 128
F32 = jnp.float32
BF16 = jnp.bfloat16
EXACT = lax.Precision.HIGHEST
ANYWHERE = pl.BlockSpec(memory_space=pl.ANY)
IN_HBM = pl.BlockSpec(memory_space=pltpu.HBM)
DEPTH = 3


def swap(value, axis, bits):
    size = lax.axis_size(axis)
    return lax.ppermute(value, axis, [(i, i ^ bits) for i in range(size)])


def exchange_rows(blocks):
    return lax.all_to_all(blocks, "expert", split_axis=0, concat_axis=0, tiled=True)


def gather_chunks(value):
    chunks = {0: value}
    bit = lax.axis_size("tensor") // 2
    while bit:
        chunks.update({s | bit: swap(c, "tensor", bit) for s, c in list(chunks.items())})
        bit //= 2
    return [chunks[s] for s in range(len(chunks))]


def scatter_rows(value, rows):
    return jnp.sum(exchange_rows(value.reshape(-1, rows, value.shape[1])).astype(F32), axis=0)


def dot(a, b, dims=((1,), (0,)), precision=None):
    return lax.dot_general(
        a, b, (dims, ((), ())), precision=precision, preferred_element_type=F32
    )


def iota(shape, dim):
    return lax.broadcasted_iota(jnp.int32, shape, dim)


def flat_rows(part):
    return part.reshape(part.shape[0] * part.shape[1], part.shape[2])


def block(index, size):
    return pl.ds(pl.multiple_of(index * size, size), size)


def placed(space, shape, dtype=BF16):
    return space(shape, dtype)


def stream(copies, step, steps):
    @pl.when(step == 0)
    def _():
        for ahead in range(min(DEPTH - 1, steps)):
            for copy in copies(ahead):
                copy.start()

    @pl.when(step + DEPTH - 1 < steps)
    def _():
        for copy in copies(step + DEPTH - 1):
            copy.start()


def gather(to_row_ref, sources, held_ref, rows_ref, sems):
    copies = [
        pltpu.make_async_copy(
            source.at[:, :, pl.ds(0, held_ref.shape[3])], held_ref.at[s], sems.at[s]
        )
        for s, source in enumerate(sources)
    ]
    for copy in copies:
        copy.start()
    for s, copy in enumerate(copies):
        copy.wait()
        rows_ref[s] = dot(to_row_ref[...], flat_rows(held_ref[s])).astype(BF16)


def pack_kernel(me_ref, token_ref, routing_ref, gates_ref, out_ref):
    _, width = token_ref.shape
    top = routing_ref.shape[1]
    gates = gates_ref[...]
    high = gates.astype(BF16)
    middle = (gates - high.astype(F32)).astype(BF16)
    low = (gates - high.astype(F32) - middle.astype(F32)).astype(BF16)
    parts = (routing_ref[...].astype(F32).astype(BF16), high, middle, low)
    lanes = (top, LANES)
    packed = sum(
        dot(part, (iota(lanes, 0) + i * top == iota(lanes, 1)).astype(F32).astype(BF16))
        for i, part in enumerate(parts)
    ).astype(BF16)
    for group in range(out_ref.shape[0]):
        out_ref[group, :, :width] = token_ref[...]
        out_ref[group, :, width:] = packed


def repeat_kernel(me_ref, token_ref, *refs):
    out_ref = refs[-1]
    for group in range(out_ref.shape[0]):
        out_ref[group] = token_ref[...]


def plan_kernel(top, local, me_ref, packed_ref, to_token_ref, to_row_ref, gate_ref):
    total, rows = to_token_ref.shape
    room = rows // local
    packed = flat_rows(packed_ref[...]).astype(F32)
    chosen = packed[:, :top]
    value = sum(packed[:, i * top : (i + 1) * top] for i in (1, 2, 3))
    lane = iota((total, local), 1)
    match = jnp.zeros((total, local), F32)
    gate = jnp.zeros((total, local), F32)
    for e in range(local):
        hit = chosen == (me_ref[1] + e).astype(F32)
        here = lane == e
        found = jnp.sum(jnp.where(hit, 1.0, 0.0), axis=1, keepdims=True)
        match = jnp.where(here, found, match)
        gate = jnp.where(here, jnp.sum(jnp.where(hit, value, 0.0), axis=1, keepdims=True), gate)
    step = min(total, 256)
    earlier = (iota((step, step), 0) > iota((step, step), 1)).astype(F32).astype(BF16)
    spread = (iota((local, rows), 1) // room == iota((local, rows), 0)).astype(F32)
    count = jnp.zeros((1, local), F32)
    gates = jnp.zeros((rows, local), F32)
    for start in range(0, total, step):
        part = match[start : start + step]
        before = dot(earlier, part.astype(BF16)) + count
        count = count + jnp.sum(part, axis=0, keepdims=True)
        place = dot(jnp.where(part > 0.0, before, -1.0), spread, precision=EXACT)
        slot = (iota((step, rows), 1) % room).astype(F32)
        one_hot = jnp.where(place == slot, 1.0, 0.0)
        to_token_ref[start : start + step, :] = one_hot.astype(BF16)
        flipped = one_hot.T
        to_row_ref[:, start : start + step] = flipped.astype(BF16)
        gates = gates + dot(flipped, gate[start : start + step], precision=EXACT)
    own = iota((rows, local), 0) // room == iota((rows, local), 1)
    gate_ref[...] = jnp.sum(jnp.where(own, gates, 0.0), axis=1, keepdims=True)


def preact_kernel(n, steps, me_ref, to_row_ref, gate_ref, *refs):
    xs, w_ref = refs[:n], refs[n]
    act_ref, spread_ref, slope_ref, held_ref, rows_ref, x_sems, buffer, sems = refs[-8:]
    room, width = act_ref.shape[0], rows_ref.shape[2]
    e = pl.program_id(0)

    def copies(step):
        slot = step % DEPTH
        return [
            pltpu.make_async_copy(
                w_ref.at[step, block(me_ref[0] ^ s, width), :], buffer.at[slot, s], sems.at[slot, s]
            )
            for s in range(n)
        ]

    stream(copies, e, steps)

    @pl.when(e == 0)
    def _():
        gather(to_row_ref, xs, held_ref, rows_ref, x_sems)

    for copy in copies(e):
        copy.wait()
    pre = sum(dot(rows_ref[s, block(e, room), :], buffer[e % DEPTH, s]) for s in range(n))
    sig = jax.nn.sigmoid(pre)
    gate = gate_ref[...]
    act = (gate * (pre * sig)).astype(BF16)
    act_ref[...] = act
    spread_ref[...] = dot(to_row_ref[block(e, room), :], act, ((0,), (0,))).astype(BF16)
    slope_ref[...] = gate * (sig * (1.0 + pre * (1.0 - sig)))


def slope_kernel(n, steps, me_ref, to_row_ref, slope_ref, *refs):
    ys, w_ref = refs[:n], refs[n]
    grad_ref, spread_ref, held_ref, rows_ref, y_sems, buffer, sems = refs[-7:]
    room, hid = grad_ref.shape
    width = rows_ref.shape[2]
    e = pl.program_id(0)

    def copies(step):
        slot = step % DEPTH
        return [
            pltpu.make_async_copy(
                w_ref.at[block(step, hid), block(me_ref[0] ^ s, width)],
                buffer.at[slot, s],
                sems.at[slot, s],
            )
            for s in range(n)
        ]

    stream(copies, e, steps)

    @pl.when(e == 0)
    def _():
        gather(to_row_ref, ys, held_ref, rows_ref, y_sems)

    for copy in copies(e):
        copy.wait()
    grad = sum(
        dot(buffer[e % DEPTH, s], rows_ref[s, block(e, room), :], ((1,), (1,))) for s in range(n)
    )
    grad = (grad.T * slope_ref[...]).astype(BF16)
    grad_ref[...] = grad
    spread_ref[...] = dot(to_row_ref[block(e, room), :], grad, ((0,), (0,))).astype(BF16)


def column_block(me_ref, step, per, odd):
    return (me_ref[0] ^ (2 * (step // per) + odd)) * per + step % per


def mix_kernel(steps, per, odd, me_ref, to_token_ref, act_ref, w_ref, *refs):
    out_ref, rows_ref, buffer, sems = refs[-4:]
    _, local, hid, cols = buffer.shape
    room = rows_ref.shape[0] // local
    step = pl.program_id(0)

    def copies(step):
        slot = step % DEPTH
        columns = block(column_block(me_ref, step, per, odd), cols)
        return [
            pltpu.make_async_copy(
                w_ref.at[pl.ds(e * hid, hid), columns], buffer.at[slot, e], sems.at[slot, e]
            )
            for e in range(local)
        ]

    stream(copies, step, steps)
    for copy in copies(step):
        copy.wait()
    for e in range(local):
        here = slice(e * room, (e + 1) * room)
        rows_ref[here, :] = dot(act_ref[here, :], buffer[step % DEPTH, e]).astype(BF16)
    out_ref[0] = dot(to_token_ref[...], rows_ref[...]).astype(BF16)


def back_kernel(steps, per, odd, me_ref, to_token_ref, grad_ref, w_ref, *refs):
    out_ref, rows_ref, buffer, sems = refs[-4:]
    _, local, cols, hid = buffer.shape
    room = rows_ref.shape[1] // local
    group = 2 if room % 128 and local % 2 == 0 else 1
    step = pl.program_id(0)

    def copies(step):
        slot = step % DEPTH
        columns = block(column_block(me_ref, step, per, odd), cols)
        return [
            pltpu.make_async_copy(
                w_ref.at[e, columns, :], buffer.at[slot, e], sems.at[slot, e]
            )
            for e in range(local)
        ]

    stream(copies, step, steps)
    for copy in copies(step):
        copy.wait()
    for first in range(0, local, group):
        part = 0.0
        for i in range(group):
            here = slice((first + i) * room, (first + i + 1) * room)
            blank = [jnp.zeros((room, hid), BF16)] * group
            blank[i] = grad_ref[here, :]
            part = part + dot(
                buffer[step % DEPTH, first + i], jnp.concatenate(blank, axis=0), ((1,), (1,))
            )
        rows_ref[:, first * room : (first + group) * room] = part.astype(BF16)
    out_ref[0] = dot(to_token_ref[...], rows_ref[...], ((1,), (1,))).astype(BF16)


def add_kernel(count, me_ref, *refs):
    parts, out_ref = refs[:count], refs[-1]
    total = sum(part[...].reshape(out_ref.shape).astype(F32) for part in parts)
    out_ref[...] = total.astype(BF16)


def drain(step, steps, out, buffer, sems):
    @pl.when(step == steps - 1)
    def _():
        for slot in range(min(2, steps)):
            for s in range(buffer.shape[1]):
                pltpu.make_async_copy(buffer.at[slot, s], out, sems.at[slot, s]).wait()


def write_step(step, steps, values, outs, buffer, sems):
    slot = step % 2

    @pl.when(step >= 2)
    def _():
        for s, out in enumerate(outs):
            pltpu.make_async_copy(buffer.at[slot, s], out, sems.at[slot, s]).wait()

    for s, value in enumerate(values()):
        buffer[slot, s] = value.astype(BF16)
    for s, out in enumerate(outs):
        pltpu.make_async_copy(buffer.at[slot, s], out, sems.at[slot, s]).start()
    drain(step, steps, outs[0], buffer, sems)


def d_out_kernel(n, steps, me_ref, act_ref, *refs):
    ys, (out_ref, done_ref, buffer, sems) = refs[:n], refs[-4:]
    e = pl.program_id(0)
    _, n, hid, width = buffer.shape
    act = act_ref[...].T
    done_ref[...] = jnp.zeros_like(done_ref)
    outs = [out_ref.at[block(e, hid), block(me_ref[0] ^ s, width)] for s in range(n)]

    def values():
        for s in range(n):
            yield dot(act, flat_rows(ys[s][...]))

    write_step(e, steps, values, outs, buffer, sems)


def d_in_kernel(n, steps, me_ref, grad_ref, *refs):
    xs, (out_ref, flipped, buffer, sems) = refs[:n], refs[-4:]
    e = pl.program_id(0)
    _, n, width, hid = buffer.shape

    @pl.when(e == 0)
    def _():
        for s in range(n):
            flipped[s] = flat_rows(xs[s][...]).T

    grad = grad_ref[...]
    outs = [out_ref.at[e, block(me_ref[0] ^ s, width), :] for s in range(n)]

    def values():
        for s in range(n):
            yield dot(flipped[s], grad)

    write_step(e, steps, values, outs, buffer, sems)


def call(kernel, name, grid, in_specs, out_specs, out_shape, args, flops, limit, scratch=(), after=()):
    moved = sum(a.size * a.dtype.itemsize for a in args)
    outs = out_shape if isinstance(out_shape, list) else [out_shape]
    moved += sum(math.prod(o.shape) * jnp.dtype(o.dtype).itemsize for o in outs)
    return pl.pallas_call(
        kernel,
        grid_spec=pltpu.PrefetchScalarGridSpec(
            num_scalar_prefetch=1,
            grid=grid,
            in_specs=in_specs + [ANYWHERE] * len(after),
            out_specs=out_specs,
            scratch_shapes=scratch,
        ),
        out_shape=out_shape,
        name=name,
        cost_estimate=pl.CostEstimate(flops=flops, bytes_accessed=moved, transcendentals=0),
        compiler_params=pltpu.CompilerParams(vmem_limit_bytes=limit * MIB),
    )(*args, *after)


def once(*shape):
    return pl.BlockSpec(shape, lambda *_: (0,) * len(shape), pipeline_mode=pl.Buffered(1))


def shards(tokens, cotangent, routing, gates, w_in, w_out):
    n = lax.axis_size("tensor")
    groups = lax.axis_size("expert")
    local, width, hid = w_in.shape
    rows, quarter = tokens.shape
    total = groups * rows
    top = routing.shape[1]
    room = groups * (rows // 4)
    slots = local * room
    tensor_index = lax.axis_index("tensor").astype(jnp.int32)
    first = lax.axis_index("expert").astype(jnp.int32) * local
    me = jnp.stack([tensor_index, first])
    big = total > 256
    flops = 2 * slots * hid * width
    limit = 56 if big else 20
    dense = jax.ShapeDtypeStruct((total, local * hid), BF16)
    packed = call(
        pack_kernel,
        "pack",
        (1,),
        [once(rows, quarter), once(rows, top), once(rows, top)],
        once(groups, rows, quarter + LANES),
        jax.ShapeDtypeStruct((groups, rows, quarter + LANES), BF16),
        (me, tokens, routing, gates),
        0,
        24 if big else 4,
    )
    left = exchange_rows(packed)
    xs = gather_chunks(left)
    whole = exchange_rows(
        call(
            repeat_kernel,
            "repeat",
            (1,),
            [once(rows, quarter)],
            once(groups, rows, quarter),
            jax.ShapeDtypeStruct((groups, rows, quarter), BF16),
            (me, cotangent),
            0,
            24 if big else 4,
            (),
            (left,),
        )
    )
    ys = gather_chunks(whole)
    to_token, to_row, gate = call(
        functools.partial(plan_kernel, top, local),
        "plan",
        (1,),
        [
            pl.BlockSpec(
                (groups, rows, LANES),
                lambda i, me: (0, 0, quarter // LANES),
                pipeline_mode=pl.Buffered(1),
            )
        ],
        [once(total, slots), once(slots, total), once(slots, 1)],
        [
            jax.ShapeDtypeStruct((total, slots), BF16),
            jax.ShapeDtypeStruct((slots, total), BF16),
            jax.ShapeDtypeStruct((slots, 1), F32),
        ],
        (me, left),
        0,
        48 if big else 6,
    )

    def ring(*shape):
        return [
            pltpu.VMEM((DEPTH, *shape), BF16),
            pltpu.SemaphoreType.DMA((DEPTH, shape[0])),
        ]

    chunk_specs = [once(groups, rows, quarter)] * n
    loose = [ANYWHERE] * n + [IN_HBM]
    row_block = pl.BlockSpec((room, hid), lambda e, me: (e, 0))
    dense_block = pl.BlockSpec((total, hid), lambda e, me: (0, e))
    row_shape = jax.ShapeDtypeStruct((slots, hid), BF16)
    gathered = [
        pltpu.VMEM((n, groups, rows, quarter), BF16),
        pltpu.VMEM((n, slots, quarter), BF16),
        pltpu.SemaphoreType.DMA((n,)),
    ]
    w_in = pltpu.with_memory_space_constraint(w_in, pltpu.HBM)
    flat_out = pltpu.with_memory_space_constraint(
        w_out.reshape(local * hid, width), pltpu.HBM
    )
    act, act_dense, slope = call(
        functools.partial(preact_kernel, n, local),
        "preact",
        (local,),
        [once(slots, total), pl.BlockSpec((room, 1), lambda e, me: (e, 0))] + loose,
        [row_block, dense_block, row_block],
        [row_shape, dense, jax.ShapeDtypeStruct((slots, hid), F32)],
        (me, to_row, gate, *xs, w_in),
        flops,
        limit,
        gathered + ring(n, quarter, hid),
        (whole,),
    )
    cols = min(512, quarter)
    per = quarter // cols
    steps = n // 2 * per

    def parts(kernel, name, held, weights, odd, after=()):
        shape = (local, hid, cols) if weights.ndim == 2 else (local, cols, hid)
        return call(
            functools.partial(kernel, steps, per, odd),
            name,
            (steps,),
            [once(total, slots), once(slots, hid), IN_HBM],
            pl.BlockSpec((1, total, cols), lambda i, me: (i // per, 0, i % per)),
            jax.ShapeDtypeStruct((n // 2, total, quarter), BF16),
            (me, to_token, held, weights),
            flops // 2,
            limit,
            [pltpu.VMEM((slots, cols) if weights.ndim == 2 else (cols, slots), BF16)] + ring(*shape),
            after,
        )

    def add(name, values, specs, after=()):
        return call(
            functools.partial(add_kernel, len(values)),
            name,
            (1,),
            specs,
            once(total, quarter),
            jax.ShapeDtypeStruct((total, quarter), BF16),
            (me, *values),
            0,
            56 if big else 8,
            (),
            after,
        )

    def one_of(index):
        shape = (1, total, quarter)
        return pl.BlockSpec(shape, lambda i, me: (index, 0, 0), pipeline_mode=pl.Buffered(1))

    def pass_on(name, even, odd):
        got = swap(odd, "tensor", 1)
        return got, {
            i: add(f"{name}_{i}", (even, got), [one_of(i), one_of(i)]) for i in range(1, n // 2)
        }

    def gather_sum(name, even, got, sent, after=()):
        values, specs = [even, got], [one_of(0), one_of(0)]
        count = n // 2
        bit = n // 2
        held = dict(sent)
        while count > 1:
            half = count // 2
            for i in range(half, count):
                received = swap(held[i], "tensor", bit)
                if i == half:
                    values.append(received)
                    specs.append(once(total, quarter))
                else:
                    held[i - half] = add(
                        f"{name}_{i - half}_{bit}",
                        (held[i - half], received),
                        [once(total, quarter)] * 2,
                    )
            count, bit = half, bit // 2
        return add(f"{name}_sum", values, specs, after)

    mix_odd = parts(mix_kernel, "mix_odd", act, flat_out, 1, (ys[n // 2],))
    mix_even = parts(mix_kernel, "mix_even", act, flat_out, 0, (mix_odd,))
    mix_got, mix_sent = pass_on("mix", mix_even, mix_odd)
    mix_sum = gather_sum("mix", mix_even, mix_got, mix_sent)
    mixed = scatter_rows(mix_sum, rows).astype(BF16)

    grad, grad_dense = call(
        functools.partial(slope_kernel, n, local),
        "grad_preact",
        (local,),
        [once(slots, total), row_block] + loose,
        [row_block, dense_block],
        [row_shape, dense],
        (me, to_row, slope, *ys, flat_out),
        flops,
        limit,
        gathered + ring(n, hid, quarter),
        tuple(mix_sent.values()),
    )

    back_odd = parts(back_kernel, "back_odd", grad, w_in, 1, (mix_sum,))
    back_even = parts(back_kernel, "back_even", grad, w_in, 0, (back_odd,))
    back_got, back_sent = pass_on("back", back_even, back_odd)

    sems = pltpu.SemaphoreType.DMA((2, n))
    d_w_out, done = call(
        functools.partial(d_out_kernel, n, local),
        "d_w_out",
        (local,),
        [dense_block] + chunk_specs,
        [IN_HBM, once(8, 128)],
        [placed(pltpu.HBM, (local * hid, width)), jax.ShapeDtypeStruct((8, 128), F32)],
        (me, act_dense, *ys),
        2 * total * local * hid * width,
        limit,
        [pltpu.VMEM((2, n, hid, quarter), BF16), sems],
        tuple(back_sent.values()),
    )
    back_sum = gather_sum("back", back_even, back_got, back_sent, (done,))
    d_tokens = scatter_rows(back_sum, rows).astype(BF16)
    d_w_in = call(
        functools.partial(d_in_kernel, n, local),
        "d_w_in",
        (local,),
        [dense_block] + chunk_specs,
        IN_HBM,
        placed(pltpu.HBM, w_in.shape),
        (me, grad_dense, *xs),
        2 * total * local * hid * width,
        limit,
        [
            pltpu.VMEM((n, quarter, total), BF16),
            pltpu.VMEM((2, n, quarter, hid), BF16),
            sems,
        ],
        (back_sum,),
    )
    return mixed, d_tokens, d_w_in, d_w_out.reshape(w_out.shape)


def solution(mesh):
    rows = P("expert", "tensor")
    routes = P("expert", None)
    columns_in = P("expert", None, "tensor")
    rows_out = P("expert", "tensor", None)
    return jax.shard_map(
        shards,
        mesh=mesh,
        in_specs=(rows, rows, routes, routes, columns_in, rows_out),
        out_specs=(rows, rows, columns_in, rows_out),
        check_vma=False,
    )
```

```python
import functools
import math

import jax
import jax.numpy as jnp
from jax import lax
from jax.experimental import pallas as pl
from jax.experimental.pallas import tpu as pltpu
from jax.sharding import PartitionSpec as P

MIB = 1024 * 1024
LANES = 128
F32 = jnp.float32
BF16 = jnp.bfloat16
EXACT = lax.Precision.HIGHEST
ANYWHERE = pl.BlockSpec(memory_space=pl.ANY)
IN_HBM = pl.BlockSpec(memory_space=pltpu.HBM)
DEPTH = 3


def swap(value, axis, bits):
    size = lax.axis_size(axis)
    return lax.ppermute(value, axis, [(i, i ^ bits) for i in range(size)])


def exchange_rows(blocks):
    return lax.all_to_all(blocks, "expert", split_axis=0, concat_axis=0, tiled=True)


def gather_chunks(value):
    chunks = {0: value}
    bit = lax.axis_size("tensor") // 2
    while bit:
        chunks.update({s | bit: swap(c, "tensor", bit) for s, c in list(chunks.items())})
        bit //= 2
    return [chunks[s] for s in range(len(chunks))]


def scatter_rows(value, rows):
    return jnp.sum(exchange_rows(value.reshape(-1, rows, value.shape[1])).astype(F32), axis=0)


def dot(a, b, dims=((1,), (0,)), precision=None):
    return lax.dot_general(
        a, b, (dims, ((), ())), precision=precision, preferred_element_type=F32
    )


def iota(shape, dim):
    return lax.broadcasted_iota(jnp.int32, shape, dim)


def flat_rows(part):
    return part.reshape(part.shape[0] * part.shape[1], part.shape[2])


def block(index, size):
    return pl.ds(pl.multiple_of(index * size, size), size)


def placed(space, shape, dtype=BF16):
    return space(shape, dtype)


def stream(copies, step, steps, depth):
    @pl.when(step == 0)
    def _():
        for ahead in range(min(depth - 1, steps)):
            for copy in copies(ahead):
                copy.start()

    @pl.when(step + depth - 1 < steps)
    def _():
        for copy in copies(step + depth - 1):
            copy.start()


def gather(to_row_ref, sources, held_ref, rows_ref, sems):
    width = held_ref.shape[3]
    copies = [
        pltpu.make_async_copy(source.at[:, :, pl.ds(start, width)], held_ref.at[s], sems.at[s])
        for s, (source, start) in enumerate(sources)
    ]
    for copy in copies:
        copy.start()
    for s, copy in enumerate(copies):
        copy.wait()
        rows_ref[s] = dot(to_row_ref[...], flat_rows(held_ref[s])).astype(BF16)


def pack_kernel(me_ref, token_ref, routing_ref, gates_ref, out_ref):
    _, width = token_ref.shape
    top = routing_ref.shape[1]
    gates = gates_ref[...]
    high = gates.astype(BF16)
    middle = (gates - high.astype(F32)).astype(BF16)
    low = (gates - high.astype(F32) - middle.astype(F32)).astype(BF16)
    parts = (routing_ref[...].astype(F32).astype(BF16), high, middle, low)
    lanes = (top, LANES)
    packed = sum(
        dot(part, (iota(lanes, 0) + i * top == iota(lanes, 1)).astype(F32).astype(BF16))
        for i, part in enumerate(parts)
    ).astype(BF16)
    for group in range(out_ref.shape[0]):
        out_ref[group, :, :width] = token_ref[...]
        out_ref[group, :, width:] = packed


def repeat_kernel(count, me_ref, *refs):
    parts, out_ref = refs[:count], refs[-1]
    width = parts[0].shape[1]
    for i, part in enumerate(parts):
        for group in range(out_ref.shape[0]):
            out_ref[group, :, i * width : (i + 1) * width] = part[...]


def plan_kernel(top, local, me_ref, packed_ref, to_token_ref, to_row_ref, gate_ref):
    total, rows = to_token_ref.shape
    room = rows // local
    packed = flat_rows(packed_ref[...]).astype(F32)
    chosen = packed[:, :top]
    value = sum(packed[:, i * top : (i + 1) * top] for i in (1, 2, 3))
    lane = iota((total, local), 1)
    match = jnp.zeros((total, local), F32)
    gate = jnp.zeros((total, local), F32)
    for e in range(local):
        hit = chosen == (me_ref[1] + e).astype(F32)
        here = lane == e
        found = jnp.sum(jnp.where(hit, 1.0, 0.0), axis=1, keepdims=True)
        match = jnp.where(here, found, match)
        gate = jnp.where(here, jnp.sum(jnp.where(hit, value, 0.0), axis=1, keepdims=True), gate)
    step = min(total, 256)
    earlier = (iota((step, step), 0) > iota((step, step), 1)).astype(F32).astype(BF16)
    spread = (iota((local, rows), 1) // room == iota((local, rows), 0)).astype(F32)
    count = jnp.zeros((1, local), F32)
    gates = jnp.zeros((rows, local), F32)
    for start in range(0, total, step):
        part = match[start : start + step]
        before = dot(earlier, part.astype(BF16)) + count
        count = count + jnp.sum(part, axis=0, keepdims=True)
        place = dot(jnp.where(part > 0.0, before, -1.0), spread, precision=EXACT)
        slot = (iota((step, rows), 1) % room).astype(F32)
        one_hot = jnp.where(place == slot, 1.0, 0.0)
        to_token_ref[start : start + step, :] = one_hot.astype(BF16)
        flipped = one_hot.T
        to_row_ref[:, start : start + step] = flipped.astype(BF16)
        gates = gates + dot(flipped, gate[start : start + step], precision=EXACT)
    own = iota((rows, local), 0) // room == iota((rows, local), 1)
    gate_ref[...] = jnp.sum(jnp.where(own, gates, 0.0), axis=1, keepdims=True)


def preact_kernel(n, steps, me_ref, to_row_ref, gate_ref, *refs):
    xs, w_ref = refs[:n], refs[n]
    act_ref, spread_ref, slope_ref, held_ref, rows_ref, x_sems, buffer, sems = refs[-8:]
    room, width, depth = act_ref.shape[0], rows_ref.shape[2], buffer.shape[0]
    e = pl.program_id(0)

    def copies(step):
        slot = step % depth
        return [
            pltpu.make_async_copy(
                w_ref.at[step, block(me_ref[0] ^ s, width), :], buffer.at[slot, s], sems.at[slot, s]
            )
            for s in range(n)
        ]

    stream(copies, e, steps, depth)

    @pl.when(e == 0)
    def _():
        gather(to_row_ref, [(x, 0) for x in xs], held_ref, rows_ref, x_sems)

    for copy in copies(e):
        copy.wait()
    pre = sum(dot(rows_ref[s, block(e, room), :], buffer[e % depth, s]) for s in range(n))
    sig = jax.nn.sigmoid(pre)
    gate = gate_ref[...]
    act = (gate * (pre * sig)).astype(BF16)
    act_ref[...] = act
    spread_ref[...] = dot(to_row_ref[block(e, room), :], act, ((0,), (0,))).astype(BF16)
    slope_ref[...] = gate * (sig * (1.0 + pre * (1.0 - sig)))


def middle_kernel(n, steps, me_ref, to_token_ref, to_row_ref, slope_ref, act_ref, *refs):
    ys, w_ref = refs[:2], refs[2]
    sums, (grad_ref, spread_ref) = refs[3:5], refs[5:7]
    held_ref, rows_ref, y_sems, out_rows_ref, buffer, sems = refs[7:]
    room, hid = grad_ref.shape
    width, depth = rows_ref.shape[2], buffer.shape[0]
    e = pl.program_id(0)

    def copies(step):
        slot = step % depth
        return [
            pltpu.make_async_copy(
                w_ref.at[block(step, hid), block(me_ref[0] ^ s, width)],
                buffer.at[slot, s],
                sems.at[slot, s],
            )
            for s in range(n)
        ]

    stream(copies, e, steps, depth)

    @pl.when(e == 0)
    def _():
        sources = [(ys[s % 2], s // 2 * width) for s in range(n)]
        gather(to_row_ref, sources, held_ref, rows_ref, y_sems)

    for copy in copies(e):
        copy.wait()
    here = block(e, room)
    grad = 0.0
    for s in range(n):
        weights = buffer[e % depth, s]
        out_rows_ref[s, here, :] = dot(act_ref[...], weights).astype(BF16)
        grad = grad + dot(weights, rows_ref[s, here, :], ((1,), (1,)))
    grad = (grad.T * slope_ref[...]).astype(BF16)
    grad_ref[...] = grad
    spread_ref[...] = dot(to_row_ref[here, :], grad, ((0,), (0,))).astype(BF16)

    @pl.when(e == steps - 1)
    def _():
        for s in range(n):
            total = dot(to_token_ref[...], out_rows_ref[s])
            sums[s % 2][s // 2] = total.astype(BF16)


def back_kernel(steps, per, odd, me_ref, to_token_ref, grad_ref, w_ref, *refs):
    out_ref, rows_ref, buffer, sems = refs[-4:]
    depth, pairs, cols, wide = buffer.shape
    hid = grad_ref.shape[1]
    group = wide // hid
    room = rows_ref.shape[1] // (pairs * group)
    step = pl.program_id(0)

    def copies(step):
        slot = step % depth
        column = (me_ref[0] ^ (2 * (step // per) + odd)) * per + step % per
        return [
            pltpu.make_async_copy(
                w_ref.at[p * group + i, block(column, cols), :],
                buffer.at[slot, p, :, pl.ds(i * hid, hid)],
                sems.at[slot, p * group + i],
            )
            for p in range(pairs)
            for i in range(group)
        ]

    stream(copies, step, steps, depth)
    for copy in copies(step):
        copy.wait()
    for p in range(pairs):
        corners = []
        for i in range(group):
            start = (p * group + i) * room
            blank = [jnp.zeros((room, hid), BF16)] * group
            blank[i] = grad_ref[start : start + room, :]
            corners.append(jnp.concatenate(blank, axis=1) if group > 1 else blank[0])
        corner = jnp.concatenate(corners, axis=0) if group > 1 else corners[0]
        part = dot(buffer[step % depth, p], corner, ((1,), (1,)))
        rows_ref[:, p * group * room : (p + 1) * group * room] = part.astype(BF16)
    out_ref[0] = dot(to_token_ref[...], rows_ref[...], ((1,), (1,))).astype(BF16)


def add_kernel(count, me_ref, *refs):
    parts, out_ref = refs[:count], refs[-1]
    total = sum(part[...].reshape(out_ref.shape).astype(F32) for part in parts)
    out_ref[...] = total.astype(BF16)


def drain(step, steps, out, buffer, sems):
    @pl.when(step == steps - 1)
    def _():
        for slot in range(min(2, steps)):
            for s in range(buffer.shape[1]):
                pltpu.make_async_copy(buffer.at[slot, s], out, sems.at[slot, s]).wait()


def write_step(step, steps, values, outs, buffer, sems):
    slot = step % 2

    @pl.when(step >= 2)
    def _():
        for s, out in enumerate(outs):
            pltpu.make_async_copy(buffer.at[slot, s], out, sems.at[slot, s]).wait()

    for s, value in enumerate(values()):
        buffer[slot, s] = value.astype(BF16)
    for s, out in enumerate(outs):
        pltpu.make_async_copy(buffer.at[slot, s], out, sems.at[slot, s]).start()
    drain(step, steps, outs[0], buffer, sems)


def d_out_kernel(n, steps, me_ref, act_ref, *refs):
    ys, (out_ref, done_ref, buffer, sems) = refs[:2], refs[-4:]
    e = pl.program_id(0)
    _, n, hid, width = buffer.shape
    act = act_ref[...].T
    done_ref[...] = jnp.zeros_like(done_ref)
    outs = [out_ref.at[block(e, hid), block(me_ref[0] ^ s, width)] for s in range(n)]

    def values():
        for s in range(n):
            start = s // 2 * width
            yield dot(act, flat_rows(ys[s % 2][:, :, start : start + width]))

    write_step(e, steps, values, outs, buffer, sems)


def d_in_kernel(n, pairs, me_ref, grad_ref, *refs):
    xs, (out_ref, flipped, buffer, sems) = refs[:n], refs[-4:]
    p, s = pl.program_id(0), pl.program_id(1)
    slots, group, width, hid = buffer.shape
    step, steps = p * n + s, pairs * n
    slot = step % slots

    for i in range(n):

        @pl.when((p == 0) & (s == i))
        def _():
            flipped[i] = flat_rows(xs[i][...]).T

    def copies(slot):
        return [
            pltpu.make_async_copy(
                buffer.at[slot, i],
                out_ref.at[p * group + i, block(me_ref[0] ^ s, width), :],
                sems.at[slot, i],
            )
            for i in range(group)
        ]

    @pl.when(step >= slots)
    def _():
        for copy in copies(slot):
            copy.wait()

    value = dot(flipped[s], grad_ref[...]).astype(BF16)
    for i, copy in enumerate(copies(slot)):
        buffer[slot, i] = value[:, i * hid : (i + 1) * hid]
        copy.start()

    @pl.when(step == steps - 1)
    def _():
        for last in range(min(slots, steps)):
            for copy in copies(last):
                copy.wait()


def call(kernel, name, grid, in_specs, out_specs, out_shape, args, flops, limit, scratch=(), after=()):
    moved = sum(a.size * a.dtype.itemsize for a in args)
    outs = out_shape if isinstance(out_shape, list) else [out_shape]
    moved += sum(math.prod(o.shape) * jnp.dtype(o.dtype).itemsize for o in outs)
    return pl.pallas_call(
        kernel,
        grid_spec=pltpu.PrefetchScalarGridSpec(
            num_scalar_prefetch=1,
            grid=grid,
            in_specs=in_specs + [ANYWHERE] * len(after),
            out_specs=out_specs,
            scratch_shapes=scratch,
        ),
        out_shape=out_shape,
        name=name,
        cost_estimate=pl.CostEstimate(flops=flops, bytes_accessed=moved, transcendentals=0),
        compiler_params=pltpu.CompilerParams(vmem_limit_bytes=limit * MIB),
    )(*args, *after)


def once(*shape):
    return pl.BlockSpec(shape, lambda *_: (0,) * len(shape), pipeline_mode=pl.Buffered(1))


def shards(tokens, cotangent, routing, gates, w_in, w_out):
    n = lax.axis_size("tensor")
    groups = lax.axis_size("expert")
    local, width, hid = w_in.shape
    rows, quarter = tokens.shape
    total = groups * rows
    top = routing.shape[1]
    room = groups * (rows // 4)
    slots = local * room
    tensor_index = lax.axis_index("tensor").astype(jnp.int32)
    first = lax.axis_index("expert").astype(jnp.int32) * local
    me = jnp.stack([tensor_index, first])
    big = total > 256
    flops = 2 * slots * hid * width
    limit = 56 if big else 20
    dense = jax.ShapeDtypeStruct((total, local * hid), BF16)
    packed = call(
        pack_kernel,
        "pack",
        (1,),
        [once(rows, quarter), once(rows, top), once(rows, top)],
        once(groups, rows, quarter + LANES),
        jax.ShapeDtypeStruct((groups, rows, quarter + LANES), BF16),
        (me, tokens, routing, gates),
        0,
        24 if big else 4,
    )
    left = exchange_rows(packed)
    xs = gather_chunks(left)
    raw = {0: cotangent}
    bit = n // 2
    while bit > 1:
        raw.update({k | bit: swap(c, "tensor", bit) for k, c in list(raw.items())})
        bit //= 2
    raw = [raw[k] for k in sorted(raw)]
    wide = len(raw) * quarter
    even_y = exchange_rows(
        call(
            functools.partial(repeat_kernel, len(raw)),
            "repeat",
            (1,),
            [once(rows, quarter)] * len(raw),
            once(groups, rows, wide),
            jax.ShapeDtypeStruct((groups, rows, wide), BF16),
            (me, *raw),
            0,
            24 if big else 6,
            (),
            (xs[1],),
        )
    )
    ys = (even_y, swap(even_y, "tensor", 1))
    to_token, to_row, gate = call(
        functools.partial(plan_kernel, top, local),
        "plan",
        (1,),
        [
            pl.BlockSpec(
                (groups, rows, LANES),
                lambda i, me: (0, 0, quarter // LANES),
                pipeline_mode=pl.Buffered(1),
            )
        ],
        [once(total, slots), once(slots, total), once(slots, 1)],
        [
            jax.ShapeDtypeStruct((total, slots), BF16),
            jax.ShapeDtypeStruct((slots, total), BF16),
            jax.ShapeDtypeStruct((slots, 1), F32),
        ],
        (me, left),
        0,
        48 if big else 6,
    )

    depth = min(DEPTH, local)

    def ring(*shape):
        return [
            pltpu.VMEM((depth, *shape), BF16),
            pltpu.SemaphoreType.DMA((depth, shape[0])),
        ]

    chunk_specs = [once(groups, rows, quarter)] * n
    loose = [ANYWHERE] * n + [IN_HBM]
    row_block = pl.BlockSpec((room, hid), lambda e, me: (e, 0))
    dense_block = pl.BlockSpec((total, hid), lambda e, me: (0, e))
    row_shape = jax.ShapeDtypeStruct((slots, hid), BF16)
    gathered = [
        pltpu.VMEM((n, groups, rows, quarter), BF16),
        pltpu.VMEM((n, slots, quarter), BF16),
        pltpu.SemaphoreType.DMA((n,)),
    ]
    w_in = pltpu.with_memory_space_constraint(w_in, pltpu.HBM)
    flat_out = pltpu.with_memory_space_constraint(
        w_out.reshape(local * hid, width), pltpu.HBM
    )
    act, act_dense, slope = call(
        functools.partial(preact_kernel, n, local),
        "preact",
        (local,),
        [once(slots, total), pl.BlockSpec((room, 1), lambda e, me: (e, 0))] + loose,
        [row_block, dense_block, row_block],
        [row_shape, dense, jax.ShapeDtypeStruct((slots, hid), F32)],
        (me, to_row, gate, *xs, w_in),
        flops,
        limit,
        gathered + ring(n, quarter, hid),
        (even_y,),
    )
    cols = min(512, quarter)
    per = quarter // cols
    steps = n // 2 * per
    group = 2 if local % 2 == 0 else 1
    sum_spec = once(n // 2, total, quarter)
    sum_shape = jax.ShapeDtypeStruct((n // 2, total, quarter), BF16)
    mix_even, mix_odd, grad, grad_dense = call(
        functools.partial(middle_kernel, n, local),
        "middle",
        (local,),
        [once(total, slots), once(slots, total), row_block, row_block]
        + [ANYWHERE] * 2
        + [IN_HBM],
        [sum_spec, sum_spec, row_block, dense_block],
        [sum_shape, sum_shape, row_shape, dense],
        (me, to_token, to_row, slope, act, *ys, flat_out),
        2 * flops,
        56 if big else 30,
        gathered + [pltpu.VMEM((n, slots, quarter), BF16)] + ring(n, hid, quarter),
    )

    def back(name, odd, after=()):
        return call(
            functools.partial(back_kernel, steps, per, odd),
            name,
            (steps,),
            [once(total, slots), once(slots, hid), IN_HBM],
            pl.BlockSpec((1, total, cols), lambda i, me: (i // per, 0, i % per)),
            sum_shape,
            (me, to_token, grad, w_in),
            flops // 2,
            limit,
            [pltpu.VMEM((cols, slots), BF16)]
            + [
                pltpu.VMEM((DEPTH, local // group, cols, group * hid), BF16),
                pltpu.SemaphoreType.DMA((DEPTH, local)),
            ],
            after,
        )

    def add(name, values, specs, after=()):
        return call(
            functools.partial(add_kernel, len(values)),
            name,
            (1,),
            specs,
            once(total, quarter),
            jax.ShapeDtypeStruct((total, quarter), BF16),
            (me, *values),
            0,
            56 if big else 8,
            (),
            after,
        )

    def one_of(index):
        shape = (1, total, quarter)
        return pl.BlockSpec(shape, lambda i, me: (index, 0, 0), pipeline_mode=pl.Buffered(1))

    def pass_on(name, even, odd, after=()):
        got = swap(odd, "tensor", 1)
        return got, {
            i: add(f"{name}_{i}", (even, got), [one_of(i), one_of(i)], after)
            for i in range(1, n // 2)
        }

    def gather_sum(name, even, got, sent, after=()):
        values, specs = [even, got], [one_of(0), one_of(0)]
        count = n // 2
        bit = n // 2
        held = dict(sent)
        while count > 1:
            half = count // 2
            for i in range(half, count):
                received = swap(held[i], "tensor", bit)
                if i == half:
                    values.append(received)
                    specs.append(once(total, quarter))
                else:
                    held[i - half] = add(
                        f"{name}_{i - half}_{bit}",
                        (held[i - half], received),
                        [once(total, quarter)] * 2,
                    )
            count, bit = half, bit // 2
        return add(f"{name}_sum", values, specs, after)

    back_odd = back("back_odd", 1)
    mix_got, mix_sent = pass_on("mix", mix_even, mix_odd, (back_odd,))
    back_even = back("back_even", 0, tuple(mix_sent.values()))
    back_got, back_sent = pass_on("back", back_even, back_odd)

    sems = pltpu.SemaphoreType.DMA((2, n))
    d_w_out, done = call(
        functools.partial(d_out_kernel, n, local),
        "d_w_out",
        (local,),
        [dense_block] + [once(groups, rows, wide)] * 2,
        [IN_HBM, once(8, 128)],
        [placed(pltpu.HBM, (local * hid, width)), jax.ShapeDtypeStruct((8, 128), F32)],
        (me, act_dense, *ys),
        2 * total * local * hid * width,
        limit,
        [pltpu.VMEM((2, n, hid, quarter), BF16), sems],
        tuple(back_sent.values()),
    )
    mix_sum = gather_sum("mix", mix_even, mix_got, mix_sent, (done,))
    mixed = scatter_rows(mix_sum, rows).astype(BF16)
    back_sum = gather_sum("back", back_even, back_got, back_sent, (mix_sum,))
    d_tokens = scatter_rows(back_sum, rows).astype(BF16)
    d_w_in = call(
        functools.partial(d_in_kernel, n, local // group),
        "d_w_in",
        (local // group, n),
        [pl.BlockSpec((total, group * hid), lambda p, s, me: (0, p))] + chunk_specs,
        IN_HBM,
        placed(pltpu.HBM, w_in.shape),
        (me, grad_dense, *xs),
        2 * total * local * hid * width,
        limit,
        [
            pltpu.VMEM((n, quarter, total), BF16),
            pltpu.VMEM((4, group, quarter, hid), BF16),
            pltpu.SemaphoreType.DMA((4, group)),
        ],
        (back_sum,),
    )
    return mixed, d_tokens, d_w_in, d_w_out.reshape(w_out.shape)


def solution(mesh):
    rows = P("expert", "tensor")
    routes = P("expert", None)
    columns_in = P("expert", None, "tensor")
    rows_out = P("expert", "tensor", None)
    return jax.shard_map(
        shards,
        mesh=mesh,
        in_specs=(rows, rows, routes, routes, columns_in, rows_out),
        out_specs=(rows, rows, columns_in, rows_out),
        check_vma=False,
    )
```

```python
import functools
import math

import jax
import jax.numpy as jnp
from jax import lax
from jax.experimental import pallas as pl
from jax.experimental.pallas import tpu as pltpu
from jax.sharding import PartitionSpec as P

MIB = 1024 * 1024
LANES = 128
F32 = jnp.float32
BF16 = jnp.bfloat16
EXACT = lax.Precision.HIGHEST
ANYWHERE = pl.BlockSpec(memory_space=pl.ANY)
IN_HBM = pl.BlockSpec(memory_space=pltpu.HBM)
DEPTH = 3


def swap(value, axis, bits):
    size = lax.axis_size(axis)
    return lax.ppermute(value, axis, [(i, i ^ bits) for i in range(size)])


def exchange_rows(blocks):
    return lax.all_to_all(blocks, "expert", split_axis=0, concat_axis=0, tiled=True)


def far_chunks(value):
    chunks = {0: value}
    bit = lax.axis_size("tensor") // 2
    while bit > 1:
        chunks.update({s | bit: swap(c, "tensor", bit) for s, c in list(chunks.items())})
        bit //= 2
    return [chunks[s] for s in sorted(chunks)]


def with_pairs(chunks):
    return [part for chunk in chunks for part in (chunk, swap(chunk, "tensor", 1))]


def scatter_rows(value, rows):
    return jnp.sum(exchange_rows(value.reshape(-1, rows, value.shape[1])).astype(F32), axis=0)


def dot(a, b, dims=((1,), (0,)), precision=None):
    return lax.dot_general(
        a, b, (dims, ((), ())), precision=precision, preferred_element_type=F32
    )


def iota(shape, dim):
    return lax.broadcasted_iota(jnp.int32, shape, dim)


def flat_rows(part):
    return part.reshape(part.shape[0] * part.shape[1], part.shape[2])


def block(index, size):
    return pl.ds(pl.multiple_of(index * size, size), size)


def placed(space, shape, dtype=BF16):
    return space(shape, dtype)


def stream(copies, step, steps, depth):
    @pl.when(step == 0)
    def _():
        for ahead in range(min(depth - 1, steps)):
            for copy in copies(ahead):
                copy.start()

    @pl.when(step + depth - 1 < steps)
    def _():
        for copy in copies(step + depth - 1):
            copy.start()


def gather(to_row_ref, sources, held_ref, rows_ref, sems):
    width = held_ref.shape[3]
    copies = [
        pltpu.make_async_copy(source.at[:, :, pl.ds(start, width)], held_ref.at[s], sems.at[s])
        for s, (source, start) in enumerate(sources)
    ]
    for copy in copies:
        copy.start()
    for s, copy in enumerate(copies):
        copy.wait()
        rows_ref[s] = dot(to_row_ref[...], flat_rows(held_ref[s])).astype(BF16)


def pack_kernel(me_ref, token_ref, cot_ref, routing_ref, gates_ref, out_ref):
    _, width = token_ref.shape
    top = routing_ref.shape[1]
    gates = gates_ref[...]
    high = gates.astype(BF16)
    middle = (gates - high.astype(F32)).astype(BF16)
    low = (gates - high.astype(F32) - middle.astype(F32)).astype(BF16)
    parts = (routing_ref[...].astype(F32).astype(BF16), high, middle, low)
    lanes = (top, LANES)
    packed = sum(
        dot(part, (iota(lanes, 0) + i * top == iota(lanes, 1)).astype(F32).astype(BF16))
        for i, part in enumerate(parts)
    ).astype(BF16)
    for group in range(out_ref.shape[0]):
        out_ref[group, :, :width] = token_ref[...]
        out_ref[group, :, width : 2 * width] = cot_ref[...]
        out_ref[group, :, 2 * width :] = packed


def plan_kernel(top, local, me_ref, packed_ref, to_token_ref, to_row_ref, gate_ref):
    total, rows = to_token_ref.shape
    room = rows // local
    packed = flat_rows(packed_ref[...]).astype(F32)
    chosen = packed[:, :top]
    value = sum(packed[:, i * top : (i + 1) * top] for i in (1, 2, 3))
    lane = iota((total, local), 1)
    match = jnp.zeros((total, local), F32)
    gate = jnp.zeros((total, local), F32)
    for e in range(local):
        hit = chosen == (me_ref[1] + e).astype(F32)
        here = lane == e
        found = jnp.sum(jnp.where(hit, 1.0, 0.0), axis=1, keepdims=True)
        match = jnp.where(here, found, match)
        gate = jnp.where(here, jnp.sum(jnp.where(hit, value, 0.0), axis=1, keepdims=True), gate)
    step = min(total, 256)
    earlier = (iota((step, step), 0) > iota((step, step), 1)).astype(F32).astype(BF16)
    spread = (iota((local, rows), 1) // room == iota((local, rows), 0)).astype(F32)
    count = jnp.zeros((1, local), F32)
    gates = jnp.zeros((rows, local), F32)
    for start in range(0, total, step):
        part = match[start : start + step]
        before = dot(earlier, part.astype(BF16)) + count
        count = count + jnp.sum(part, axis=0, keepdims=True)
        place = dot(jnp.where(part > 0.0, before, -1.0), spread, precision=EXACT)
        slot = (iota((step, rows), 1) % room).astype(F32)
        one_hot = jnp.where(place == slot, 1.0, 0.0)
        to_token_ref[start : start + step, :] = one_hot.astype(BF16)
        flipped = one_hot.T
        to_row_ref[:, start : start + step] = flipped.astype(BF16)
        gates = gates + dot(flipped, gate[start : start + step], precision=EXACT)
    own = iota((rows, local), 0) // room == iota((rows, local), 1)
    gate_ref[...] = jnp.sum(jnp.where(own, gates, 0.0), axis=1, keepdims=True)


def early_kernel(count, steps, me_ref, to_row_ref, *refs):
    xs, w_ref = refs[:count], refs[count]
    part_ref, held_ref, rows_ref, x_sems, buffer, sems = refs[count + 1 :]
    room, width, depth = part_ref.shape[0], rows_ref.shape[2], buffer.shape[0]
    e = pl.program_id(0)

    def copies(step):
        slot = step % depth
        return [
            pltpu.make_async_copy(
                w_ref.at[step, block(me_ref[0] ^ s, width), :], buffer.at[slot, s], sems.at[slot, s]
            )
            for s in range(count)
        ]

    stream(copies, e, steps, depth)

    @pl.when(e == 0)
    def _():
        gather(to_row_ref, [(x, 0) for x in xs], held_ref, rows_ref, x_sems)

    for copy in copies(e):
        copy.wait()
    part_ref[...] = sum(
        dot(rows_ref[s, block(e, room), :], buffer[e % depth, s]) for s in range(count)
    )


def front_kernel(
    n, begin, steps, me_ref, to_token_ref, to_row_ref, gate_ref, part_ref, *refs
):
    count = n - begin
    xs, w_in_ref, w_out_ref = refs[:count], refs[count], refs[count + 1]
    act_ref, spread_ref, slope_ref = refs[count + 2 : count + 5]
    sums = refs[count + 5 : count + 7]
    held_ref, rows_ref, x_sems, out_rows_ref = refs[count + 7 : count + 11]
    in_buffer, in_sems, out_buffer, out_sems = refs[count + 11 :]
    room, hid = act_ref.shape
    width, depth = rows_ref.shape[2], in_buffer.shape[0]
    e = pl.program_id(0)

    def in_copies(step):
        slot = step % depth
        return [
            pltpu.make_async_copy(
                w_in_ref.at[step, block(me_ref[0] ^ (begin + i), width), :],
                in_buffer.at[slot, i],
                in_sems.at[slot, i],
            )
            for i in range(count)
        ]

    def out_copies(step):
        slot = step % depth
        return [
            pltpu.make_async_copy(
                w_out_ref.at[block(step, hid), block(me_ref[0] ^ s, width)],
                out_buffer.at[slot, s],
                out_sems.at[slot, s],
            )
            for s in range(n)
        ]

    stream(lambda step: in_copies(step) + out_copies(step), e, steps, depth)

    @pl.when(e == 0)
    def _():
        gather(to_row_ref, [(x, 0) for x in xs], held_ref, rows_ref, x_sems)

    here = block(e, room)
    for copy in in_copies(e):
        copy.wait()
    pre = part_ref[...]
    for i in range(count):
        pre = pre + dot(rows_ref[i, here, :], in_buffer[e % depth, i])
    sig = jax.nn.sigmoid(pre)
    gate = gate_ref[...]
    act = (gate * (pre * sig)).astype(BF16)
    act_ref[...] = act
    spread_ref[...] = dot(to_row_ref[here, :], act, ((0,), (0,))).astype(BF16)
    slope_ref[...] = gate * (sig * (1.0 + pre * (1.0 - sig)))
    for s, copy in enumerate(out_copies(e)):
        copy.wait()
        out_rows_ref[s, here, :] = dot(act, out_buffer[e % depth, s]).astype(BF16)

    @pl.when(e == steps - 1)
    def _():
        for s in range(n):
            total = dot(to_token_ref[...], out_rows_ref[s])
            sums[s % 2][s // 2] = total.astype(BF16)


def slope_kernel(n, steps, me_ref, to_row_ref, slope_ref, *refs):
    ys, w_ref = refs[:n], refs[n]
    grad_ref, spread_ref, held_ref, rows_ref, y_sems, buffer, sems = refs[-7:]
    room, hid = grad_ref.shape
    width, depth = rows_ref.shape[2], buffer.shape[0]
    e = pl.program_id(0)

    def copies(step):
        slot = step % depth
        return [
            pltpu.make_async_copy(
                w_ref.at[block(step, hid), block(me_ref[0] ^ s, width)],
                buffer.at[slot, s],
                sems.at[slot, s],
            )
            for s in range(n)
        ]

    stream(copies, e, steps, depth)

    @pl.when(e == 0)
    def _():
        gather(to_row_ref, [(y, 0) for y in ys], held_ref, rows_ref, y_sems)

    here = block(e, room)
    grad = 0.0
    for s, copy in enumerate(copies(e)):
        copy.wait()
        grad = grad + dot(buffer[e % depth, s], rows_ref[s, here, :], ((1,), (1,)))
    grad = (grad.T * slope_ref[...]).astype(BF16)
    grad_ref[...] = grad
    spread_ref[...] = dot(to_row_ref[here, :], grad, ((0,), (0,))).astype(BF16)


def back_kernel(steps, per, me_ref, to_token_ref, grad_ref, w_ref, *refs):
    odd_ref, even_ref, rows_ref, buffer, sems = refs[-5:]
    depth, pairs, cols, wide = buffer.shape
    hid = grad_ref.shape[1]
    group = wide // hid
    room = rows_ref.shape[1] // (pairs * group)
    step = pl.program_id(0)
    half = steps // 2

    def copies(step):
        slot = step % depth
        late = (step >= half).astype(jnp.int32) if not isinstance(step, int) else int(step >= half)
        inside = step - late * half
        column = (me_ref[0] ^ (2 * (inside // per) + 1 - late)) * per + inside % per
        return [
            pltpu.make_async_copy(
                w_ref.at[p * group + i, block(column, cols), :],
                buffer.at[slot, p, :, pl.ds(i * hid, hid)],
                sems.at[slot, p * group + i],
            )
            for p in range(pairs)
            for i in range(group)
        ]

    stream(copies, step, steps, depth)
    for copy in copies(step):
        copy.wait()
    for p in range(pairs):
        corners = []
        for i in range(group):
            start = (p * group + i) * room
            blank = [jnp.zeros((room, hid), BF16)] * group
            blank[i] = grad_ref[start : start + room, :]
            corners.append(jnp.concatenate(blank, axis=1) if group > 1 else blank[0])
        corner = jnp.concatenate(corners, axis=0) if group > 1 else corners[0]
        part = dot(buffer[step % depth, p], corner, ((1,), (1,)))
        rows_ref[:, p * group * room : (p + 1) * group * room] = part.astype(BF16)
    total = dot(to_token_ref[...], rows_ref[...], ((1,), (1,))).astype(BF16)

    @pl.when(step < half)
    def _():
        odd_ref[0] = total

    @pl.when(step >= half)
    def _():
        even_ref[0] = total


def add_kernel(count, me_ref, *refs):
    parts, out_ref = refs[:count], refs[-1]
    total = sum(part[...].reshape(out_ref.shape).astype(F32) for part in parts)
    out_ref[...] = total.astype(BF16)


def drain(step, steps, out, buffer, sems):
    @pl.when(step == steps - 1)
    def _():
        for slot in range(min(2, steps)):
            for s in range(buffer.shape[1]):
                pltpu.make_async_copy(buffer.at[slot, s], out, sems.at[slot, s]).wait()


def write_step(step, steps, values, outs, buffer, sems):
    slot = step % 2

    @pl.when(step >= 2)
    def _():
        for s, out in enumerate(outs):
            pltpu.make_async_copy(buffer.at[slot, s], out, sems.at[slot, s]).wait()

    for s, value in enumerate(values()):
        buffer[slot, s] = value.astype(BF16)
    for s, out in enumerate(outs):
        pltpu.make_async_copy(buffer.at[slot, s], out, sems.at[slot, s]).start()
    drain(step, steps, outs[0], buffer, sems)


def d_out_kernel(n, steps, me_ref, act_ref, *refs):
    ys, (out_ref, done_ref, buffer, sems) = refs[:n], refs[-4:]
    e = pl.program_id(0)
    _, n, hid, width = buffer.shape
    act = act_ref[...].T
    done_ref[...] = jnp.zeros_like(done_ref)
    outs = [out_ref.at[block(e, hid), block(me_ref[0] ^ s, width)] for s in range(n)]

    def values():
        for s in range(n):
            yield dot(act, flat_rows(ys[s][...]))

    write_step(e, steps, values, outs, buffer, sems)


def d_in_kernel(n, pairs, me_ref, grad_ref, *refs):
    xs, (out_ref, flipped, buffer, sems) = refs[:n], refs[-4:]
    p, s = pl.program_id(0), pl.program_id(1)
    slots, group, width, hid = buffer.shape
    step, steps = p * n + s, pairs * n
    slot = step % slots

    for i in range(n):

        @pl.when((p == 0) & (s == i))
        def _():
            flipped[i] = flat_rows(xs[i][...]).T

    def copies(slot):
        return [
            pltpu.make_async_copy(
                buffer.at[slot, i],
                out_ref.at[p * group + i, block(me_ref[0] ^ s, width), :],
                sems.at[slot, i],
            )
            for i in range(group)
        ]

    @pl.when(step >= slots)
    def _():
        for copy in copies(slot):
            copy.wait()

    value = dot(flipped[s], grad_ref[...]).astype(BF16)
    for i, copy in enumerate(copies(slot)):
        buffer[slot, i] = value[:, i * hid : (i + 1) * hid]
        copy.start()

    @pl.when(step == steps - 1)
    def _():
        for last in range(min(slots, steps)):
            for copy in copies(last):
                copy.wait()


def call(kernel, name, grid, in_specs, out_specs, out_shape, args, flops, limit, scratch=(), after=()):
    moved = sum(a.size * a.dtype.itemsize for a in args)
    outs = out_shape if isinstance(out_shape, list) else [out_shape]
    moved += sum(math.prod(o.shape) * jnp.dtype(o.dtype).itemsize for o in outs)
    return pl.pallas_call(
        kernel,
        grid_spec=pltpu.PrefetchScalarGridSpec(
            num_scalar_prefetch=1,
            grid=grid,
            in_specs=in_specs + [ANYWHERE] * len(after),
            out_specs=out_specs,
            scratch_shapes=scratch,
        ),
        out_shape=out_shape,
        name=name,
        cost_estimate=pl.CostEstimate(flops=flops, bytes_accessed=moved, transcendentals=0),
        compiler_params=pltpu.CompilerParams(vmem_limit_bytes=limit * MIB),
    )(*args, *after)


def once(*shape):
    return pl.BlockSpec(shape, lambda *_: (0,) * len(shape), pipeline_mode=pl.Buffered(1))


def shards(tokens, cotangent, routing, gates, w_in, w_out):
    n = lax.axis_size("tensor")
    groups = lax.axis_size("expert")
    local, width, hid = w_in.shape
    rows, quarter = tokens.shape
    total = groups * rows
    top = routing.shape[1]
    room = groups * (rows // 4)
    slots = local * room
    tensor_index = lax.axis_index("tensor").astype(jnp.int32)
    first = lax.axis_index("expert").astype(jnp.int32) * local
    me = jnp.stack([tensor_index, first])
    big = total > 256
    flops = 2 * slots * hid * width
    limit = 56 if big else 20
    dense = jax.ShapeDtypeStruct((total, local * hid), BF16)
    packed = call(
        pack_kernel,
        "pack",
        (1,),
        [once(rows, quarter)] * 2 + [once(rows, top)] * 2,
        once(groups, rows, 2 * quarter + LANES),
        jax.ShapeDtypeStruct((groups, rows, 2 * quarter + LANES), BF16),
        (me, tokens, cotangent, routing, gates),
        0,
        32 if big else 6,
    )
    left = exchange_rows(packed)
    x_far = far_chunks(left[:, :, :quarter])
    x_near = [x_far[0], swap(x_far[0], "tensor", 1)]
    ys = with_pairs(far_chunks(left[:, :, quarter : 2 * quarter]))
    to_token, to_row, gate = call(
        functools.partial(plan_kernel, top, local),
        "plan",
        (1,),
        [
            pl.BlockSpec(
                (groups, rows, LANES),
                lambda i, me: (0, 0, 2 * quarter // LANES),
                pipeline_mode=pl.Buffered(1),
            )
        ],
        [once(total, slots), once(slots, total), once(slots, 1)],
        [
            jax.ShapeDtypeStruct((total, slots), BF16),
            jax.ShapeDtypeStruct((slots, total), BF16),
            jax.ShapeDtypeStruct((slots, 1), F32),
        ],
        (me, left),
        0,
        48 if big else 6,
    )

    depth = min(DEPTH, local)

    def ring(*shape):
        return [
            pltpu.VMEM((depth, *shape), BF16),
            pltpu.SemaphoreType.DMA((depth, shape[0])),
        ]

    chunk_specs = [once(groups, rows, quarter)] * n
    row_block = pl.BlockSpec((room, hid), lambda e, me: (e, 0))
    dense_block = pl.BlockSpec((total, hid), lambda e, me: (0, e))
    row_shape = jax.ShapeDtypeStruct((slots, hid), BF16)

    def gathered(count):
        return [
            pltpu.VMEM((count, groups, rows, quarter), BF16),
            pltpu.VMEM((count, slots, quarter), BF16),
            pltpu.SemaphoreType.DMA((count,)),
        ]

    w_in = pltpu.with_memory_space_constraint(w_in, pltpu.HBM)
    flat_out = pltpu.with_memory_space_constraint(
        w_out.reshape(local * hid, width), pltpu.HBM
    )
    begin = len(x_near)
    part = call(
        functools.partial(early_kernel, begin, local),
        "preact_early",
        (local,),
        [once(slots, total)] + [ANYWHERE] * begin + [IN_HBM],
        row_block,
        jax.ShapeDtypeStruct((slots, hid), F32),
        (me, to_row, *x_near, w_in),
        flops // 2,
        limit,
        gathered(begin) + ring(begin, quarter, hid),
    )
    *x_far, part = lax.optimization_barrier((*x_far[1:], part))
    xs = x_near + with_pairs(x_far)
    sum_spec = once(n // 2, total, quarter)
    sum_shape = jax.ShapeDtypeStruct((n // 2, total, quarter), BF16)
    act, act_dense, slope, mix_even, mix_odd = call(
        functools.partial(front_kernel, n, begin, local),
        "front",
        (local,),
        [
            once(total, slots),
            once(slots, total),
            pl.BlockSpec((room, 1), lambda e, me: (e, 0)),
            row_block,
        ]
        + [ANYWHERE] * (n - begin)
        + [IN_HBM] * 2,
        [row_block, dense_block, row_block, sum_spec, sum_spec],
        [row_shape, dense, jax.ShapeDtypeStruct((slots, hid), F32), sum_shape, sum_shape],
        (me, to_token, to_row, gate, part, *xs[begin:], w_in, flat_out),
        2 * flops,
        56 if big else 30,
        gathered(n - begin)
        + [pltpu.VMEM((n, slots, quarter), BF16)]
        + ring(n - begin, quarter, hid)
        + ring(n, hid, quarter),
    )
    grad, grad_dense = call(
        functools.partial(slope_kernel, n, local),
        "grad_preact",
        (local,),
        [once(slots, total), row_block] + [ANYWHERE] * n + [IN_HBM],
        [row_block, dense_block],
        [row_shape, dense],
        (me, to_row, slope, *ys, flat_out),
        flops,
        limit,
        gathered(n) + ring(n, hid, quarter),
    )
    cols = min(512, quarter)
    per = quarter // cols
    steps = n * per
    half = steps // 2
    group = 2 if local % 2 == 0 else 1

    def odd_block(i, me):
        i = jnp.minimum(i, half - 1)
        return i // per, 0, i % per

    def even_block(i, me):
        i = jnp.maximum(i - half, 0)
        return i // per, 0, i % per

    def back(after):
        return call(
            functools.partial(back_kernel, steps, per),
            "back",
            (steps,),
            [once(total, slots), once(slots, hid), IN_HBM],
            [pl.BlockSpec((1, total, cols), odd_block), pl.BlockSpec((1, total, cols), even_block)],
            [sum_shape, sum_shape],
            (me, to_token, grad, w_in),
            flops,
            limit,
            [pltpu.VMEM((cols, slots), BF16)]
            + [
                pltpu.VMEM((DEPTH, local // group, cols, group * hid), BF16),
                pltpu.SemaphoreType.DMA((DEPTH, local)),
            ],
            after,
        )

    def add(name, values, specs, after=()):
        return call(
            functools.partial(add_kernel, len(values)),
            name,
            (1,),
            specs,
            once(total, quarter),
            jax.ShapeDtypeStruct((total, quarter), BF16),
            (me, *values),
            0,
            56 if big else 8,
            (),
            after,
        )

    def one_of(index):
        shape = (1, total, quarter)
        return pl.BlockSpec(shape, lambda i, me: (index, 0, 0), pipeline_mode=pl.Buffered(1))

    def pass_on(name, even, odd, after=()):
        got = swap(odd, "tensor", 1)
        return got, {
            i: add(f"{name}_{i}", (even, got), [one_of(i), one_of(i)], after)
            for i in range(1, n // 2)
        }

    def gather_sum(name, even, got, sent, after=()):
        values, specs = [even, got], [one_of(0), one_of(0)]
        count = n // 2
        bit = n // 2
        held = dict(sent)
        while count > 1:
            half = count // 2
            for i in range(half, count):
                received = swap(held[i], "tensor", bit)
                if i == half:
                    values.append(received)
                    specs.append(once(total, quarter))
                else:
                    held[i - half] = add(
                        f"{name}_{i - half}_{bit}",
                        (held[i - half], received),
                        [once(total, quarter)] * 2,
                    )
            count, bit = half, bit // 2
        return add(f"{name}_sum", values, specs, after)

    mix_got, mix_sent = pass_on("mix", mix_even, mix_odd, (grad,))
    back_odd, back_even = back(tuple(mix_sent.values()))
    mix_sum = gather_sum("mix", mix_even, mix_got, mix_sent, (back_odd,))
    mixed = scatter_rows(mix_sum, rows).astype(BF16)
    back_got, back_sent = pass_on("back", back_even, back_odd, (mix_sum,))

    sems = pltpu.SemaphoreType.DMA((2, n))
    d_w_out, done = call(
        functools.partial(d_out_kernel, n, local),
        "d_w_out",
        (local,),
        [dense_block] + chunk_specs,
        [IN_HBM, once(8, 128)],
        [placed(pltpu.HBM, (local * hid, width)), jax.ShapeDtypeStruct((8, 128), F32)],
        (me, act_dense, *ys),
        2 * total * local * hid * width,
        limit,
        [pltpu.VMEM((2, n, hid, quarter), BF16), sems],
        tuple(back_sent.values()),
    )
    back_sum = gather_sum("back", back_even, back_got, back_sent, (done,))
    d_tokens = scatter_rows(back_sum, rows).astype(BF16)
    d_w_in = call(
        functools.partial(d_in_kernel, n, local // group),
        "d_w_in",
        (local // group, n),
        [pl.BlockSpec((total, group * hid), lambda p, s, me: (0, p))] + chunk_specs,
        IN_HBM,
        placed(pltpu.HBM, w_in.shape),
        (me, grad_dense, *xs),
        2 * total * local * hid * width,
        limit,
        [
            pltpu.VMEM((n, quarter, total), BF16),
            pltpu.VMEM((4, group, quarter, hid), BF16),
            pltpu.SemaphoreType.DMA((4, group)),
        ],
        (back_sum,),
    )
    return mixed, d_tokens, d_w_in, d_w_out.reshape(w_out.shape)


def solution(mesh):
    rows = P("expert", "tensor")
    routes = P("expert", None)
    columns_in = P("expert", None, "tensor")
    rows_out = P("expert", "tensor", None)
    return jax.shard_map(
        shards,
        mesh=mesh,
        in_specs=(rows, rows, routes, routes, columns_in, rows_out),
        out_specs=(rows, rows, columns_in, rows_out),
        check_vma=False,
    )
```

```python
import functools
import math

import jax
import jax.numpy as jnp
from jax import lax
from jax.experimental import pallas as pl
from jax.experimental.pallas import tpu as pltpu
from jax.sharding import PartitionSpec as P

MIB = 1024 * 1024
LANES = 128
F32 = jnp.float32
BF16 = jnp.bfloat16
EXACT = lax.Precision.HIGHEST
ANYWHERE = pl.BlockSpec(memory_space=pl.ANY)
IN_HBM = pl.BlockSpec(memory_space=pltpu.HBM)
DEPTH = 3


def swap(value, axis, bits):
    size = lax.axis_size(axis)
    return lax.ppermute(value, axis, [(i, i ^ bits) for i in range(size)])


def exchange_rows(blocks):
    return lax.all_to_all(blocks, "expert", split_axis=0, concat_axis=0, tiled=True)


def gather_chunks(value):
    chunks = {0: value}
    bit = lax.axis_size("tensor") // 2
    while bit:
        chunks.update({s | bit: swap(c, "tensor", bit) for s, c in list(chunks.items())})
        bit //= 2
    return [chunks[s] for s in range(len(chunks))]


def far_chunks(value):
    chunks = {0: value}
    bit = lax.axis_size("tensor") // 2
    while bit > 1:
        chunks.update({s | bit: swap(c, "tensor", bit) for s, c in list(chunks.items())})
        bit //= 2
    return [chunks[s] for s in sorted(chunks)]


def scatter_rows(value, rows):
    return jnp.sum(exchange_rows(value.reshape(-1, rows, value.shape[1])).astype(F32), axis=0)


def dot(a, b, dims=((1,), (0,)), precision=None):
    return lax.dot_general(
        a, b, (dims, ((), ())), precision=precision, preferred_element_type=F32
    )


def iota(shape, dim):
    return lax.broadcasted_iota(jnp.int32, shape, dim)


def flat_rows(part):
    return part.reshape(part.shape[0] * part.shape[1], part.shape[2])


def block(index, size):
    return pl.ds(pl.multiple_of(index * size, size), size)


def placed(space, shape, dtype=BF16):
    return space(shape, dtype)


def stream(copies, step, steps, depth):
    @pl.when(step == 0)
    def _():
        for ahead in range(min(depth - 1, steps)):
            for copy in copies(ahead):
                copy.start()

    @pl.when(step + depth - 1 < steps)
    def _():
        for copy in copies(step + depth - 1):
            copy.start()


def gather(to_row_ref, sources, held_ref, rows_ref, sems):
    width = held_ref.shape[3]
    copies = [
        pltpu.make_async_copy(source.at[:, :, pl.ds(start, width)], held_ref.at[s], sems.at[s])
        for s, (source, start) in enumerate(sources)
    ]
    for copy in copies:
        copy.start()
    for s, copy in enumerate(copies):
        copy.wait()
        rows_ref[s] = dot(to_row_ref[...], flat_rows(held_ref[s])).astype(BF16)


def pack_kernel(me_ref, token_ref, routing_ref, gates_ref, out_ref):
    _, width = token_ref.shape
    top = routing_ref.shape[1]
    gates = gates_ref[...]
    high = gates.astype(BF16)
    middle = (gates - high.astype(F32)).astype(BF16)
    low = (gates - high.astype(F32) - middle.astype(F32)).astype(BF16)
    parts = (routing_ref[...].astype(F32).astype(BF16), high, middle, low)
    lanes = (top, LANES)
    packed = sum(
        dot(part, (iota(lanes, 0) + i * top == iota(lanes, 1)).astype(F32).astype(BF16))
        for i, part in enumerate(parts)
    ).astype(BF16)
    for group in range(out_ref.shape[0]):
        out_ref[group, :, :width] = token_ref[...]
        out_ref[group, :, width:] = packed


def repeat_kernel(me_ref, token_ref, *refs):
    out_ref = refs[-1]
    for group in range(out_ref.shape[0]):
        out_ref[group] = token_ref[...]


def plan_kernel(top, local, me_ref, packed_ref, to_token_ref, to_row_ref, gate_ref):
    total, rows = to_token_ref.shape
    room = rows // local
    packed = flat_rows(packed_ref[...]).astype(F32)
    chosen = packed[:, :top]
    value = sum(packed[:, i * top : (i + 1) * top] for i in (1, 2, 3))
    lane = iota((total, local), 1)
    match = jnp.zeros((total, local), F32)
    gate = jnp.zeros((total, local), F32)
    for e in range(local):
        hit = chosen == (me_ref[1] + e).astype(F32)
        here = lane == e
        found = jnp.sum(jnp.where(hit, 1.0, 0.0), axis=1, keepdims=True)
        match = jnp.where(here, found, match)
        gate = jnp.where(here, jnp.sum(jnp.where(hit, value, 0.0), axis=1, keepdims=True), gate)
    step = min(total, 256)
    earlier = (iota((step, step), 0) > iota((step, step), 1)).astype(F32).astype(BF16)
    spread = (iota((local, rows), 1) // room == iota((local, rows), 0)).astype(F32)
    count = jnp.zeros((1, local), F32)
    gates = jnp.zeros((rows, local), F32)
    for start in range(0, total, step):
        part = match[start : start + step]
        before = dot(earlier, part.astype(BF16)) + count
        count = count + jnp.sum(part, axis=0, keepdims=True)
        place = dot(jnp.where(part > 0.0, before, -1.0), spread, precision=EXACT)
        slot = (iota((step, rows), 1) % room).astype(F32)
        one_hot = jnp.where(place == slot, 1.0, 0.0)
        to_token_ref[start : start + step, :] = one_hot.astype(BF16)
        flipped = one_hot.T
        to_row_ref[:, start : start + step] = flipped.astype(BF16)
        gates = gates + dot(flipped, gate[start : start + step], precision=EXACT)
    own = iota((rows, local), 0) // room == iota((rows, local), 1)
    gate_ref[...] = jnp.sum(jnp.where(own, gates, 0.0), axis=1, keepdims=True)


def preact_kernel(n, steps, me_ref, to_row_ref, gate_ref, *refs):
    xs, w_ref = refs[:n], refs[n]
    act_ref, spread_ref, slope_ref, held_ref, rows_ref, x_sems, buffer, sems = refs[-8:]
    room, width, depth = act_ref.shape[0], rows_ref.shape[2], buffer.shape[0]
    e = pl.program_id(0)

    def copies(step):
        slot = step % depth
        return [
            pltpu.make_async_copy(
                w_ref.at[step, block(me_ref[0] ^ s, width), :], buffer.at[slot, s], sems.at[slot, s]
            )
            for s in range(n)
        ]

    stream(copies, e, steps, depth)

    @pl.when(e == 0)
    def _():
        gather(to_row_ref, [(x, 0) for x in xs], held_ref, rows_ref, x_sems)

    for copy in copies(e):
        copy.wait()
    pre = sum(dot(rows_ref[s, block(e, room), :], buffer[e % depth, s]) for s in range(n))
    sig = jax.nn.sigmoid(pre)
    gate = gate_ref[...]
    act = (gate * (pre * sig)).astype(BF16)
    act_ref[...] = act
    spread_ref[...] = dot(to_row_ref[block(e, room), :], act, ((0,), (0,))).astype(BF16)
    slope_ref[...] = gate * (sig * (1.0 + pre * (1.0 - sig)))


def middle_kernel(n, steps, me_ref, to_token_ref, to_row_ref, slope_ref, act_ref, *refs):
    ys, w_ref = refs[:n], refs[n]
    sums, (grad_ref, spread_ref) = refs[n + 1 : n + 3], refs[n + 3 : n + 5]
    held_ref, rows_ref, y_sems, out_rows_ref, buffer, sems = refs[n + 5 :]
    room, hid = grad_ref.shape
    width, depth = rows_ref.shape[2], buffer.shape[0]
    e = pl.program_id(0)

    def copies(step):
        slot = step % depth
        return [
            pltpu.make_async_copy(
                w_ref.at[block(step, hid), block(me_ref[0] ^ s, width)],
                buffer.at[slot, s],
                sems.at[slot, s],
            )
            for s in range(n)
        ]

    stream(copies, e, steps, depth)

    @pl.when(e == 0)
    def _():
        gather(to_row_ref, [(y, 0) for y in ys], held_ref, rows_ref, y_sems)

    for copy in copies(e):
        copy.wait()
    here = block(e, room)
    grad = 0.0
    for s in range(n):
        weights = buffer[e % depth, s]
        out_rows_ref[s, here, :] = dot(act_ref[...], weights).astype(BF16)
        grad = grad + dot(weights, rows_ref[s, here, :], ((1,), (1,)))
    grad = (grad.T * slope_ref[...]).astype(BF16)
    grad_ref[...] = grad
    spread_ref[...] = dot(to_row_ref[here, :], grad, ((0,), (0,))).astype(BF16)

    @pl.when(e == steps - 1)
    def _():
        for s in range(n):
            total = dot(to_token_ref[...], out_rows_ref[s])
            sums[s % 2][s // 2] = total.astype(BF16)


def back_kernel(steps, per, odd, me_ref, to_token_ref, grad_ref, w_ref, *refs):
    out_ref, rows_ref, buffer, sems = refs[-4:]
    depth, pairs, cols, wide = buffer.shape
    hid = grad_ref.shape[1]
    group = wide // hid
    room = rows_ref.shape[1] // (pairs * group)
    step = pl.program_id(0)

    def copies(step):
        slot = step % depth
        column = (me_ref[0] ^ (2 * (step // per) + odd)) * per + step % per
        return [
            pltpu.make_async_copy(
                w_ref.at[p * group + i, block(column, cols), :],
                buffer.at[slot, p, :, pl.ds(i * hid, hid)],
                sems.at[slot, p * group + i],
            )
            for p in range(pairs)
            for i in range(group)
        ]

    stream(copies, step, steps, depth)
    for copy in copies(step):
        copy.wait()
    for p in range(pairs):
        corners = []
        for i in range(group):
            start = (p * group + i) * room
            blank = [jnp.zeros((room, hid), BF16)] * group
            blank[i] = grad_ref[start : start + room, :]
            corners.append(jnp.concatenate(blank, axis=1) if group > 1 else blank[0])
        corner = jnp.concatenate(corners, axis=0) if group > 1 else corners[0]
        part = dot(buffer[step % depth, p], corner, ((1,), (1,)))
        rows_ref[:, p * group * room : (p + 1) * group * room] = part.astype(BF16)
    out_ref[0] = dot(to_token_ref[...], rows_ref[...], ((1,), (1,))).astype(BF16)


def add_kernel(count, me_ref, *refs):
    parts, out_ref = refs[:count], refs[-1]
    total = sum(part[...].reshape(out_ref.shape).astype(F32) for part in parts)
    out_ref[...] = total.astype(BF16)


def drain(step, steps, out, buffer, sems):
    @pl.when(step == steps - 1)
    def _():
        for slot in range(min(2, steps)):
            for s in range(buffer.shape[1]):
                pltpu.make_async_copy(buffer.at[slot, s], out, sems.at[slot, s]).wait()


def write_step(step, steps, values, outs, buffer, sems):
    slot = step % 2

    @pl.when(step >= 2)
    def _():
        for s, out in enumerate(outs):
            pltpu.make_async_copy(buffer.at[slot, s], out, sems.at[slot, s]).wait()

    for s, value in enumerate(values()):
        buffer[slot, s] = value.astype(BF16)
    for s, out in enumerate(outs):
        pltpu.make_async_copy(buffer.at[slot, s], out, sems.at[slot, s]).start()
    drain(step, steps, outs[0], buffer, sems)


def d_out_kernel(n, steps, me_ref, act_ref, *refs):
    ys, (out_ref, done_ref, buffer, sems) = refs[:n], refs[-4:]
    e = pl.program_id(0)
    _, n, hid, width = buffer.shape
    act = act_ref[...].T
    done_ref[...] = jnp.zeros_like(done_ref)
    outs = [out_ref.at[block(e, hid), block(me_ref[0] ^ s, width)] for s in range(n)]

    def values():
        for s in range(n):
            yield dot(act, flat_rows(ys[s][...]))

    write_step(e, steps, values, outs, buffer, sems)


def d_in_kernel(n, pairs, me_ref, grad_ref, *refs):
    xs, (out_ref, flipped, buffer, sems) = refs[:n], refs[-4:]
    p, s = pl.program_id(0), pl.program_id(1)
    slots, group, width, hid = buffer.shape
    step, steps = p * n + s, pairs * n
    slot = step % slots

    for i in range(n):

        @pl.when((p == 0) & (s == i))
        def _():
            flipped[i] = flat_rows(xs[i][...]).T

    def copies(slot):
        return [
            pltpu.make_async_copy(
                buffer.at[slot, i],
                out_ref.at[p * group + i, block(me_ref[0] ^ s, width), :],
                sems.at[slot, i],
            )
            for i in range(group)
        ]

    @pl.when(step >= slots)
    def _():
        for copy in copies(slot):
            copy.wait()

    value = dot(flipped[s], grad_ref[...]).astype(BF16)
    for i, copy in enumerate(copies(slot)):
        buffer[slot, i] = value[:, i * hid : (i + 1) * hid]
        copy.start()

    @pl.when(step == steps - 1)
    def _():
        for last in range(min(slots, steps)):
            for copy in copies(last):
                copy.wait()


def call(kernel, name, grid, in_specs, out_specs, out_shape, args, flops, limit, scratch=(), after=()):
    moved = sum(a.size * a.dtype.itemsize for a in args)
    outs = out_shape if isinstance(out_shape, list) else [out_shape]
    moved += sum(math.prod(o.shape) * jnp.dtype(o.dtype).itemsize for o in outs)
    return pl.pallas_call(
        kernel,
        grid_spec=pltpu.PrefetchScalarGridSpec(
            num_scalar_prefetch=1,
            grid=grid,
            in_specs=in_specs + [ANYWHERE] * len(after),
            out_specs=out_specs,
            scratch_shapes=scratch,
        ),
        out_shape=out_shape,
        name=name,
        cost_estimate=pl.CostEstimate(flops=flops, bytes_accessed=moved, transcendentals=0),
        compiler_params=pltpu.CompilerParams(vmem_limit_bytes=limit * MIB),
    )(*args, *after)


def once(*shape):
    return pl.BlockSpec(shape, lambda *_: (0,) * len(shape), pipeline_mode=pl.Buffered(1))


def shards(tokens, cotangent, routing, gates, w_in, w_out):
    n = lax.axis_size("tensor")
    groups = lax.axis_size("expert")
    local, width, hid = w_in.shape
    rows, quarter = tokens.shape
    total = groups * rows
    top = routing.shape[1]
    room = groups * (rows // 4)
    slots = local * room
    tensor_index = lax.axis_index("tensor").astype(jnp.int32)
    first = lax.axis_index("expert").astype(jnp.int32) * local
    me = jnp.stack([tensor_index, first])
    big = total > 256
    flops = 2 * slots * hid * width
    limit = 56 if big else 20
    dense = jax.ShapeDtypeStruct((total, local * hid), BF16)
    packed = call(
        pack_kernel,
        "pack",
        (1,),
        [once(rows, quarter), once(rows, top), once(rows, top)],
        once(groups, rows, quarter + LANES),
        jax.ShapeDtypeStruct((groups, rows, quarter + LANES), BF16),
        (me, tokens, routing, gates),
        0,
        24 if big else 4,
    )
    left = exchange_rows(packed)
    xs = gather_chunks(left)
    whole = exchange_rows(
        call(
            repeat_kernel,
            "repeat",
            (1,),
            [once(rows, quarter)],
            once(groups, rows, quarter),
            jax.ShapeDtypeStruct((groups, rows, quarter), BF16),
            (me, cotangent),
            0,
            24 if big else 4,
            (),
            (left,),
        )
    )
    far = far_chunks(whole)
    to_token, to_row, gate = call(
        functools.partial(plan_kernel, top, local),
        "plan",
        (1,),
        [
            pl.BlockSpec(
                (groups, rows, LANES),
                lambda i, me: (0, 0, quarter // LANES),
                pipeline_mode=pl.Buffered(1),
            )
        ],
        [once(total, slots), once(slots, total), once(slots, 1)],
        [
            jax.ShapeDtypeStruct((total, slots), BF16),
            jax.ShapeDtypeStruct((slots, total), BF16),
            jax.ShapeDtypeStruct((slots, 1), F32),
        ],
        (me, left),
        0,
        48 if big else 6,
    )

    depth = min(DEPTH, local)

    def ring(*shape):
        return [
            pltpu.VMEM((depth, *shape), BF16),
            pltpu.SemaphoreType.DMA((depth, shape[0])),
        ]

    chunk_specs = [once(groups, rows, quarter)] * n
    loose = [ANYWHERE] * n + [IN_HBM]
    row_block = pl.BlockSpec((room, hid), lambda e, me: (e, 0))
    dense_block = pl.BlockSpec((total, hid), lambda e, me: (0, e))
    row_shape = jax.ShapeDtypeStruct((slots, hid), BF16)
    gathered = [
        pltpu.VMEM((n, groups, rows, quarter), BF16),
        pltpu.VMEM((n, slots, quarter), BF16),
        pltpu.SemaphoreType.DMA((n,)),
    ]
    w_in = pltpu.with_memory_space_constraint(w_in, pltpu.HBM)
    flat_out = pltpu.with_memory_space_constraint(
        w_out.reshape(local * hid, width), pltpu.HBM
    )
    act, act_dense, slope = call(
        functools.partial(preact_kernel, n, local),
        "preact",
        (local,),
        [once(slots, total), pl.BlockSpec((room, 1), lambda e, me: (e, 0))] + loose,
        [row_block, dense_block, row_block],
        [row_shape, dense, jax.ShapeDtypeStruct((slots, hid), F32)],
        (me, to_row, gate, *xs, w_in),
        flops,
        limit,
        gathered + ring(n, quarter, hid),
        (whole,),
    )
    near = swap(whole, "tensor", 1)
    *far, act = lax.optimization_barrier((*far[1:], act))
    ys = [whole, near]
    for chunk in far:
        ys += [chunk, swap(chunk, "tensor", 1)]
    cols = min(512, quarter)
    per = quarter // cols
    steps = n // 2 * per
    group = 2 if local % 2 == 0 else 1
    sum_spec = once(n // 2, total, quarter)
    sum_shape = jax.ShapeDtypeStruct((n // 2, total, quarter), BF16)
    mix_even, mix_odd, grad, grad_dense = call(
        functools.partial(middle_kernel, n, local),
        "middle",
        (local,),
        [once(total, slots), once(slots, total), row_block, row_block]
        + [ANYWHERE] * n
        + [IN_HBM],
        [sum_spec, sum_spec, row_block, dense_block],
        [sum_shape, sum_shape, row_shape, dense],
        (me, to_token, to_row, slope, act, *ys, flat_out),
        2 * flops,
        56 if big else 30,
        gathered + [pltpu.VMEM((n, slots, quarter), BF16)] + ring(n, hid, quarter),
    )

    def back(name, odd, after=()):
        return call(
            functools.partial(back_kernel, steps, per, odd),
            name,
            (steps,),
            [once(total, slots), once(slots, hid), IN_HBM],
            pl.BlockSpec((1, total, cols), lambda i, me: (i // per, 0, i % per)),
            sum_shape,
            (me, to_token, grad, w_in),
            flops // 2,
            limit,
            [pltpu.VMEM((cols, slots), BF16)]
            + [
                pltpu.VMEM((DEPTH, local // group, cols, group * hid), BF16),
                pltpu.SemaphoreType.DMA((DEPTH, local)),
            ],
            after,
        )

    def add(name, values, specs, after=()):
        return call(
            functools.partial(add_kernel, len(values)),
            name,
            (1,),
            specs,
            once(total, quarter),
            jax.ShapeDtypeStruct((total, quarter), BF16),
            (me, *values),
            0,
            56 if big else 8,
            (),
            after,
        )

    def one_of(index):
        shape = (1, total, quarter)
        return pl.BlockSpec(shape, lambda i, me: (index, 0, 0), pipeline_mode=pl.Buffered(1))

    def pass_on(name, even, odd, after=()):
        got = swap(odd, "tensor", 1)
        return got, {
            i: add(f"{name}_{i}", (even, got), [one_of(i), one_of(i)], after)
            for i in range(1, n // 2)
        }

    def gather_sum(name, even, got, sent, after=()):
        values, specs = [even, got], [one_of(0), one_of(0)]
        count = n // 2
        bit = n // 2
        held = dict(sent)
        while count > 1:
            half = count // 2
            for i in range(half, count):
                received = swap(held[i], "tensor", bit)
                if i == half:
                    values.append(received)
                    specs.append(once(total, quarter))
                else:
                    held[i - half] = add(
                        f"{name}_{i - half}_{bit}",
                        (held[i - half], received),
                        [once(total, quarter)] * 2,
                    )
            count, bit = half, bit // 2
        return add(f"{name}_sum", values, specs, after)

    back_odd = back("back_odd", 1)
    mix_got, mix_sent = pass_on("mix", mix_even, mix_odd, (back_odd,))
    back_even = back("back_even", 0, tuple(mix_sent.values()))
    back_got, back_sent = pass_on("back", back_even, back_odd)

    sems = pltpu.SemaphoreType.DMA((2, n))
    d_w_out, done = call(
        functools.partial(d_out_kernel, n, local),
        "d_w_out",
        (local,),
        [dense_block] + chunk_specs,
        [IN_HBM, once(8, 128)],
        [placed(pltpu.HBM, (local * hid, width)), jax.ShapeDtypeStruct((8, 128), F32)],
        (me, act_dense, *ys),
        2 * total * local * hid * width,
        limit,
        [pltpu.VMEM((2, n, hid, quarter), BF16), sems],
        tuple(back_sent.values()),
    )
    mix_sum = gather_sum("mix", mix_even, mix_got, mix_sent, (done,))
    mixed = scatter_rows(mix_sum, rows).astype(BF16)
    back_sum = gather_sum("back", back_even, back_got, back_sent, (done,))
    d_tokens = scatter_rows(back_sum, rows).astype(BF16)
    d_w_in = call(
        functools.partial(d_in_kernel, n, local // group),
        "d_w_in",
        (local // group, n),
        [pl.BlockSpec((total, group * hid), lambda p, s, me: (0, p))] + chunk_specs,
        IN_HBM,
        placed(pltpu.HBM, w_in.shape),
        (me, grad_dense, *xs),
        2 * total * local * hid * width,
        limit,
        [
            pltpu.VMEM((n, quarter, total), BF16),
            pltpu.VMEM((4, group, quarter, hid), BF16),
            pltpu.SemaphoreType.DMA((4, group)),
        ],
        (back_sum, mix_sum),
    )
    return mixed, d_tokens, d_w_in, d_w_out.reshape(w_out.shape)


def solution(mesh):
    rows = P("expert", "tensor")
    routes = P("expert", None)
    columns_in = P("expert", None, "tensor")
    rows_out = P("expert", "tensor", None)
    return jax.shard_map(
        shards,
        mesh=mesh,
        in_specs=(rows, rows, routes, routes, columns_in, rows_out),
        out_specs=(rows, rows, columns_in, rows_out),
        check_vma=False,
    )
```

```python
import functools
import math

import jax
import jax.numpy as jnp
from jax import lax
from jax.experimental import pallas as pl
from jax.experimental.pallas import tpu as pltpu
from jax.sharding import PartitionSpec as P

MIB = 1024 * 1024
LANES = 128
F32 = jnp.float32
BF16 = jnp.bfloat16
EXACT = lax.Precision.HIGHEST
ANYWHERE = pl.BlockSpec(memory_space=pl.ANY)
IN_HBM = pl.BlockSpec(memory_space=pltpu.HBM)
DEPTH = 3


def swap(value, axis, bits):
    size = lax.axis_size(axis)
    return lax.ppermute(value, axis, [(i, i ^ bits) for i in range(size)])


def exchange_rows(blocks):
    return lax.all_to_all(blocks, "expert", split_axis=0, concat_axis=0, tiled=True)


def gather_chunks(value):
    chunks = {0: value}
    bit = lax.axis_size("tensor") // 2
    while bit:
        chunks.update({s | bit: swap(c, "tensor", bit) for s, c in list(chunks.items())})
        bit //= 2
    return [chunks[s] for s in range(len(chunks))]


def far_chunks(value):
    chunks = {0: value}
    bit = lax.axis_size("tensor") // 2
    while bit > 1:
        chunks.update({s | bit: swap(c, "tensor", bit) for s, c in list(chunks.items())})
        bit //= 2
    return [chunks[s] for s in sorted(chunks)]


def scatter_rows(value, rows):
    return jnp.sum(exchange_rows(value.reshape(-1, rows, value.shape[1])).astype(F32), axis=0)


def dot(a, b, dims=((1,), (0,)), precision=None):
    return lax.dot_general(
        a, b, (dims, ((), ())), precision=precision, preferred_element_type=F32
    )


def iota(shape, dim):
    return lax.broadcasted_iota(jnp.int32, shape, dim)


def flat_rows(part):
    return part.reshape(part.shape[0] * part.shape[1], part.shape[2])


def block(index, size):
    return pl.ds(pl.multiple_of(index * size, size), size)


def placed(space, shape, dtype=BF16):
    return space(shape, dtype)


def stream(copies, step, steps, depth):
    @pl.when(step == 0)
    def _():
        for ahead in range(min(depth - 1, steps)):
            for copy in copies(ahead):
                copy.start()

    @pl.when(step + depth - 1 < steps)
    def _():
        for copy in copies(step + depth - 1):
            copy.start()


def gather(to_row_ref, sources, held_ref, rows_ref, sems):
    width = held_ref.shape[3]
    copies = [
        pltpu.make_async_copy(source.at[:, :, pl.ds(start, width)], held_ref.at[s], sems.at[s])
        for s, (source, start) in enumerate(sources)
    ]
    for copy in copies:
        copy.start()
    for s, copy in enumerate(copies):
        copy.wait()
        rows_ref[s] = dot(to_row_ref[...], flat_rows(held_ref[s])).astype(BF16)


def pack_kernel(me_ref, token_ref, routing_ref, gates_ref, out_ref):
    _, width = token_ref.shape
    top = routing_ref.shape[1]
    gates = gates_ref[...]
    high = gates.astype(BF16)
    middle = (gates - high.astype(F32)).astype(BF16)
    low = (gates - high.astype(F32) - middle.astype(F32)).astype(BF16)
    parts = (routing_ref[...].astype(F32).astype(BF16), high, middle, low)
    lanes = (top, LANES)
    packed = sum(
        dot(part, (iota(lanes, 0) + i * top == iota(lanes, 1)).astype(F32).astype(BF16))
        for i, part in enumerate(parts)
    ).astype(BF16)
    for group in range(out_ref.shape[0]):
        out_ref[group, :, :width] = token_ref[...]
        out_ref[group, :, width:] = packed


def repeat_kernel(me_ref, token_ref, *refs):
    out_ref = refs[-1]
    for group in range(out_ref.shape[0]):
        out_ref[group] = token_ref[...]


def plan_kernel(top, local, me_ref, packed_ref, to_token_ref, to_row_ref, gate_ref):
    total, rows = to_token_ref.shape
    room = rows // local
    packed = flat_rows(packed_ref[...]).astype(F32)
    chosen = packed[:, :top]
    value = sum(packed[:, i * top : (i + 1) * top] for i in (1, 2, 3))
    lane = iota((total, local), 1)
    match = jnp.zeros((total, local), F32)
    gate = jnp.zeros((total, local), F32)
    for e in range(local):
        hit = chosen == (me_ref[1] + e).astype(F32)
        here = lane == e
        found = jnp.sum(jnp.where(hit, 1.0, 0.0), axis=1, keepdims=True)
        match = jnp.where(here, found, match)
        gate = jnp.where(here, jnp.sum(jnp.where(hit, value, 0.0), axis=1, keepdims=True), gate)
    step = min(total, 256)
    earlier = (iota((step, step), 0) > iota((step, step), 1)).astype(F32).astype(BF16)
    spread = (iota((local, rows), 1) // room == iota((local, rows), 0)).astype(F32)
    count = jnp.zeros((1, local), F32)
    gates = jnp.zeros((rows, local), F32)
    for start in range(0, total, step):
        part = match[start : start + step]
        before = dot(earlier, part.astype(BF16)) + count
        count = count + jnp.sum(part, axis=0, keepdims=True)
        place = dot(jnp.where(part > 0.0, before, -1.0), spread, precision=EXACT)
        slot = (iota((step, rows), 1) % room).astype(F32)
        one_hot = jnp.where(place == slot, 1.0, 0.0)
        to_token_ref[start : start + step, :] = one_hot.astype(BF16)
        flipped = one_hot.T
        to_row_ref[:, start : start + step] = flipped.astype(BF16)
        gates = gates + dot(flipped, gate[start : start + step], precision=EXACT)
    own = iota((rows, local), 0) // room == iota((rows, local), 1)
    gate_ref[...] = jnp.sum(jnp.where(own, gates, 0.0), axis=1, keepdims=True)


def preact_kernel(n, steps, me_ref, to_row_ref, gate_ref, *refs):
    xs, w_ref = refs[:n], refs[n]
    act_ref, spread_ref, slope_ref, held_ref, rows_ref, x_sems, buffer, sems = refs[-8:]
    room, width, depth = act_ref.shape[0], rows_ref.shape[2], buffer.shape[0]
    e = pl.program_id(0)

    def copies(step):
        slot = step % depth
        return [
            pltpu.make_async_copy(
                w_ref.at[step, block(me_ref[0] ^ s, width), :], buffer.at[slot, s], sems.at[slot, s]
            )
            for s in range(n)
        ]

    stream(copies, e, steps, depth)

    @pl.when(e == 0)
    def _():
        gather(to_row_ref, [(x, 0) for x in xs], held_ref, rows_ref, x_sems)

    for copy in copies(e):
        copy.wait()
    pre = sum(dot(rows_ref[s, block(e, room), :], buffer[e % depth, s]) for s in range(n))
    sig = jax.nn.sigmoid(pre)
    gate = gate_ref[...]
    act = (gate * (pre * sig)).astype(BF16)
    act_ref[...] = act
    spread_ref[...] = dot(to_row_ref[block(e, room), :], act, ((0,), (0,))).astype(BF16)
    slope_ref[...] = gate * (sig * (1.0 + pre * (1.0 - sig)))


def middle_kernel(n, steps, me_ref, to_token_ref, to_row_ref, slope_ref, act_ref, *refs):
    ys, w_ref = refs[:n], refs[n]
    sums, (grad_ref, spread_ref) = refs[n + 1 : n + 3], refs[n + 3 : n + 5]
    held_ref, rows_ref, y_sems, out_rows_ref, buffer, sems = refs[n + 5 :]
    room, hid = grad_ref.shape
    width, depth = rows_ref.shape[2], buffer.shape[0]
    e = pl.program_id(0)

    def copies(step):
        slot = step % depth
        return [
            pltpu.make_async_copy(
                w_ref.at[block(step, hid), block(me_ref[0] ^ s, width)],
                buffer.at[slot, s],
                sems.at[slot, s],
            )
            for s in range(n)
        ]

    stream(copies, e, steps, depth)

    @pl.when(e == 0)
    def _():
        gather(to_row_ref, [(y, 0) for y in ys], held_ref, rows_ref, y_sems)

    for copy in copies(e):
        copy.wait()
    here = block(e, room)
    grad = 0.0
    for s in range(n):
        weights = buffer[e % depth, s]
        out_rows_ref[s, here, :] = dot(act_ref[...], weights).astype(BF16)
        grad = grad + dot(weights, rows_ref[s, here, :], ((1,), (1,)))
    grad = (grad.T * slope_ref[...]).astype(BF16)
    grad_ref[...] = grad
    spread_ref[...] = dot(to_row_ref[here, :], grad, ((0,), (0,))).astype(BF16)

    @pl.when(e == steps - 1)
    def _():
        for s in range(n):
            total = dot(to_token_ref[...], out_rows_ref[s])
            sums[s % 2][s // 2] = total.astype(BF16)


def back_kernel(steps, per, odd, me_ref, to_token_ref, grad_ref, w_ref, *refs):
    out_ref, rows_ref, buffer, sems = refs[-4:]
    depth, pairs, cols, wide = buffer.shape
    hid = grad_ref.shape[1]
    group = wide // hid
    room = rows_ref.shape[1] // (pairs * group)
    step = pl.program_id(0)

    def copies(step):
        slot = step % depth
        column = (me_ref[0] ^ (2 * (step // per) + odd)) * per + step % per
        return [
            pltpu.make_async_copy(
                w_ref.at[p * group + i, block(column, cols), :],
                buffer.at[slot, p, :, pl.ds(i * hid, hid)],
                sems.at[slot, p * group + i],
            )
            for p in range(pairs)
            for i in range(group)
        ]

    stream(copies, step, steps, depth)
    for copy in copies(step):
        copy.wait()
    for p in range(pairs):
        corners = []
        for i in range(group):
            start = (p * group + i) * room
            blank = [jnp.zeros((room, hid), BF16)] * group
            blank[i] = grad_ref[start : start + room, :]
            corners.append(jnp.concatenate(blank, axis=1) if group > 1 else blank[0])
        corner = jnp.concatenate(corners, axis=0) if group > 1 else corners[0]
        part = dot(buffer[step % depth, p], corner, ((1,), (1,)))
        rows_ref[:, p * group * room : (p + 1) * group * room] = part.astype(BF16)
    out_ref[0] = dot(to_token_ref[...], rows_ref[...], ((1,), (1,))).astype(BF16)


def add_kernel(count, me_ref, *refs):
    parts, out_ref = refs[:count], refs[-1]
    total = sum(part[...].reshape(out_ref.shape).astype(F32) for part in parts)
    out_ref[...] = total.astype(BF16)


def drain(step, steps, out, buffer, sems):
    @pl.when(step == steps - 1)
    def _():
        for slot in range(min(2, steps)):
            for s in range(buffer.shape[1]):
                pltpu.make_async_copy(buffer.at[slot, s], out, sems.at[slot, s]).wait()


def write_step(step, steps, values, outs, buffer, sems):
    slot = step % 2

    @pl.when(step >= 2)
    def _():
        for s, out in enumerate(outs):
            pltpu.make_async_copy(buffer.at[slot, s], out, sems.at[slot, s]).wait()

    for s, value in enumerate(values()):
        buffer[slot, s] = value.astype(BF16)
    for s, out in enumerate(outs):
        pltpu.make_async_copy(buffer.at[slot, s], out, sems.at[slot, s]).start()
    drain(step, steps, outs[0], buffer, sems)


def d_out_kernel(n, steps, me_ref, act_ref, *refs):
    ys, (out_ref, done_ref, buffer, sems) = refs[:n], refs[-4:]
    e = pl.program_id(0)
    _, n, hid, width = buffer.shape
    act = act_ref[...].T
    done_ref[...] = jnp.zeros_like(done_ref)
    outs = [out_ref.at[block(e, hid), block(me_ref[0] ^ s, width)] for s in range(n)]

    def values():
        for s in range(n):
            yield dot(act, flat_rows(ys[s][...]))

    write_step(e, steps, values, outs, buffer, sems)


def d_in_kernel(n, pairs, me_ref, grad_ref, *refs):
    xs, (out_ref, flipped, buffer, sems) = refs[:n], refs[-4:]
    p, s = pl.program_id(0), pl.program_id(1)
    slots, group, width, hid = buffer.shape
    step, steps = p * n + s, pairs * n
    slot = step % slots

    for i in range(n):

        @pl.when((p == 0) & (s == i))
        def _():
            flipped[i] = flat_rows(xs[i][...]).T

    def copies(slot):
        return [
            pltpu.make_async_copy(
                buffer.at[slot, i],
                out_ref.at[p * group + i, block(me_ref[0] ^ s, width), :],
                sems.at[slot, i],
            )
            for i in range(group)
        ]

    @pl.when(step >= slots)
    def _():
        for copy in copies(slot):
            copy.wait()

    value = dot(flipped[s], grad_ref[...]).astype(BF16)
    for i, copy in enumerate(copies(slot)):
        buffer[slot, i] = value[:, i * hid : (i + 1) * hid]
        copy.start()

    @pl.when(step == steps - 1)
    def _():
        for last in range(min(slots, steps)):
            for copy in copies(last):
                copy.wait()


def call(kernel, name, grid, in_specs, out_specs, out_shape, args, flops, limit, scratch=(), after=()):
    moved = sum(a.size * a.dtype.itemsize for a in args)
    outs = out_shape if isinstance(out_shape, list) else [out_shape]
    moved += sum(math.prod(o.shape) * jnp.dtype(o.dtype).itemsize for o in outs)
    return pl.pallas_call(
        kernel,
        grid_spec=pltpu.PrefetchScalarGridSpec(
            num_scalar_prefetch=1,
            grid=grid,
            in_specs=in_specs + [ANYWHERE] * len(after),
            out_specs=out_specs,
            scratch_shapes=scratch,
        ),
        out_shape=out_shape,
        name=name,
        cost_estimate=pl.CostEstimate(flops=flops, bytes_accessed=moved, transcendentals=0),
        compiler_params=pltpu.CompilerParams(vmem_limit_bytes=limit * MIB),
    )(*args, *after)


def once(*shape):
    return pl.BlockSpec(shape, lambda *_: (0,) * len(shape), pipeline_mode=pl.Buffered(1))


def shards(tokens, cotangent, routing, gates, w_in, w_out):
    n = lax.axis_size("tensor")
    groups = lax.axis_size("expert")
    local, width, hid = w_in.shape
    rows, quarter = tokens.shape
    total = groups * rows
    top = routing.shape[1]
    room = groups * (rows // 4)
    slots = local * room
    tensor_index = lax.axis_index("tensor").astype(jnp.int32)
    first = lax.axis_index("expert").astype(jnp.int32) * local
    me = jnp.stack([tensor_index, first])
    big = total > 256
    flops = 2 * slots * hid * width
    limit = 56 if big else 20
    dense = jax.ShapeDtypeStruct((total, local * hid), BF16)
    packed = call(
        pack_kernel,
        "pack",
        (1,),
        [once(rows, quarter), once(rows, top), once(rows, top)],
        once(groups, rows, quarter + LANES),
        jax.ShapeDtypeStruct((groups, rows, quarter + LANES), BF16),
        (me, tokens, routing, gates),
        0,
        24 if big else 4,
    )
    left = exchange_rows(packed)
    xs = gather_chunks(left)
    whole = exchange_rows(
        call(
            repeat_kernel,
            "repeat",
            (1,),
            [once(rows, quarter)],
            once(groups, rows, quarter),
            jax.ShapeDtypeStruct((groups, rows, quarter), BF16),
            (me, cotangent),
            0,
            24 if big else 4,
            (),
            (left,),
        )
    )
    far = far_chunks(whole)
    to_token, to_row, gate = call(
        functools.partial(plan_kernel, top, local),
        "plan",
        (1,),
        [
            pl.BlockSpec(
                (groups, rows, LANES),
                lambda i, me: (0, 0, quarter // LANES),
                pipeline_mode=pl.Buffered(1),
            )
        ],
        [once(total, slots), once(slots, total), once(slots, 1)],
        [
            jax.ShapeDtypeStruct((total, slots), BF16),
            jax.ShapeDtypeStruct((slots, total), BF16),
            jax.ShapeDtypeStruct((slots, 1), F32),
        ],
        (me, left),
        0,
        48 if big else 6,
    )

    depth = min(DEPTH, local)

    def ring(*shape):
        return [
            pltpu.VMEM((depth, *shape), BF16),
            pltpu.SemaphoreType.DMA((depth, shape[0])),
        ]

    chunk_specs = [once(groups, rows, quarter)] * n
    loose = [ANYWHERE] * n + [IN_HBM]
    row_block = pl.BlockSpec((room, hid), lambda e, me: (e, 0))
    dense_block = pl.BlockSpec((total, hid), lambda e, me: (0, e))
    row_shape = jax.ShapeDtypeStruct((slots, hid), BF16)
    gathered = [
        pltpu.VMEM((n, groups, rows, quarter), BF16),
        pltpu.VMEM((n, slots, quarter), BF16),
        pltpu.SemaphoreType.DMA((n,)),
    ]
    w_in = pltpu.with_memory_space_constraint(w_in, pltpu.HBM)
    flat_out = pltpu.with_memory_space_constraint(
        w_out.reshape(local * hid, width), pltpu.HBM
    )
    act, act_dense, slope = call(
        functools.partial(preact_kernel, n, local),
        "preact",
        (local,),
        [once(slots, total), pl.BlockSpec((room, 1), lambda e, me: (e, 0))] + loose,
        [row_block, dense_block, row_block],
        [row_shape, dense, jax.ShapeDtypeStruct((slots, hid), F32)],
        (me, to_row, gate, *xs, w_in),
        flops,
        limit,
        gathered + ring(n, quarter, hid),
        (whole,),
    )
    near = swap(whole, "tensor", 1)
    *far, act = lax.optimization_barrier((*far[1:], act))
    ys = [whole, near]
    for chunk in far:
        ys += [chunk, swap(chunk, "tensor", 1)]
    cols = min(512, quarter)
    per = quarter // cols
    steps = n // 2 * per
    group = 2 if local % 2 == 0 else 1
    sum_spec = once(n // 2, total, quarter)
    sum_shape = jax.ShapeDtypeStruct((n // 2, total, quarter), BF16)
    mix_even, mix_odd, grad, grad_dense = call(
        functools.partial(middle_kernel, n, local),
        "middle",
        (local,),
        [once(total, slots), once(slots, total), row_block, row_block]
        + [ANYWHERE] * n
        + [IN_HBM],
        [sum_spec, sum_spec, row_block, dense_block],
        [sum_shape, sum_shape, row_shape, placed(pltpu.HBM, dense.shape)],
        (me, to_token, to_row, slope, act, *ys, flat_out),
        2 * flops,
        56 if big else 30,
        gathered + [pltpu.VMEM((n, slots, quarter), BF16)] + ring(n, hid, quarter),
    )

    def back(name, odd, after=()):
        return call(
            functools.partial(back_kernel, steps, per, odd),
            name,
            (steps,),
            [once(total, slots), once(slots, hid), IN_HBM],
            pl.BlockSpec((1, total, cols), lambda i, me: (i // per, 0, i % per)),
            sum_shape,
            (me, to_token, grad, w_in),
            flops // 2,
            limit,
            [pltpu.VMEM((cols, slots), BF16)]
            + [
                pltpu.VMEM((DEPTH, local // group, cols, group * hid), BF16),
                pltpu.SemaphoreType.DMA((DEPTH, local)),
            ],
            after,
        )

    def add(name, values, specs, after=()):
        return call(
            functools.partial(add_kernel, len(values)),
            name,
            (1,),
            specs,
            once(total, quarter),
            jax.ShapeDtypeStruct((total, quarter), BF16),
            (me, *values),
            0,
            56 if big else 8,
            (),
            after,
        )

    def one_of(index):
        shape = (1, total, quarter)
        return pl.BlockSpec(shape, lambda i, me: (index, 0, 0), pipeline_mode=pl.Buffered(1))

    def pass_on(name, even, odd, after=()):
        got = swap(odd, "tensor", 1)
        return got, {
            i: add(f"{name}_{i}", (even, got), [one_of(i), one_of(i)], after)
            for i in range(1, n // 2)
        }

    def gather_sum(name, even, got, sent, after=()):
        values, specs = [even, got], [one_of(0), one_of(0)]
        count = n // 2
        bit = n // 2
        held = dict(sent)
        while count > 1:
            half = count // 2
            for i in range(half, count):
                received = swap(held[i], "tensor", bit)
                if i == half:
                    values.append(received)
                    specs.append(once(total, quarter))
                else:
                    held[i - half] = add(
                        f"{name}_{i - half}_{bit}",
                        (held[i - half], received),
                        [once(total, quarter)] * 2,
                    )
            count, bit = half, bit // 2
        return add(f"{name}_sum", values, specs, after)

    back_odd = back("back_odd", 1)
    mix_got, mix_sent = pass_on("mix", mix_even, mix_odd, (back_odd,))
    back_even = back("back_even", 0, tuple(mix_sent.values()))
    mix_sum = gather_sum("mix", mix_even, mix_got, mix_sent)
    mixed = scatter_rows(mix_sum, rows).astype(BF16)
    back_got, back_sent = pass_on("back", back_even, back_odd)

    sems = pltpu.SemaphoreType.DMA((2, n))
    d_w_out, done = call(
        functools.partial(d_out_kernel, n, local),
        "d_w_out",
        (local,),
        [dense_block] + chunk_specs,
        [IN_HBM, once(8, 128)],
        [placed(pltpu.HBM, (local * hid, width)), jax.ShapeDtypeStruct((8, 128), F32)],
        (me, act_dense, *ys),
        2 * total * local * hid * width,
        limit,
        [pltpu.VMEM((2, n, hid, quarter), BF16), sems],
        (*back_sent.values(), mix_sum),
    )
    back_sum = gather_sum("back", back_even, back_got, back_sent, (done,))
    d_tokens = scatter_rows(back_sum, rows).astype(BF16)
    d_w_in = call(
        functools.partial(d_in_kernel, n, local // group),
        "d_w_in",
        (local // group, n),
        [pl.BlockSpec((total, group * hid), lambda p, s, me: (0, p))] + chunk_specs,
        IN_HBM,
        placed(pltpu.HBM, w_in.shape),
        (me, grad_dense, *[pltpu.with_memory_space_constraint(x, pltpu.HBM) for x in xs]),
        2 * total * local * hid * width,
        limit,
        [
            pltpu.VMEM((n, quarter, total), BF16),
            pltpu.VMEM((4, group, quarter, hid), BF16),
            pltpu.SemaphoreType.DMA((4, group)),
        ],
        (back_sum,),
    )
    return mixed, d_tokens, d_w_in, d_w_out.reshape(w_out.shape)


def solution(mesh):
    rows = P("expert", "tensor")
    routes = P("expert", None)
    columns_in = P("expert", None, "tensor")
    rows_out = P("expert", "tensor", None)
    return jax.shard_map(
        shards,
        mesh=mesh,
        in_specs=(rows, rows, routes, routes, columns_in, rows_out),
        out_specs=(rows, rows, columns_in, rows_out),
        check_vma=False,
    )
```
